32 devices in a mesh: group: 2 (over y), box: 4 (over z), row: 2 (over x), freq: 2 (over core).
Axes of the slice: x: 2, y: 2, z: 4, core: 2. Of those that a mesh axis runs over, the one named last changes fastest.
Arguments:
- base_maps: float32 [16, 4, 2, 256, 256], P(('group', 'box'), 'freq'), parts along dimension 0, may hold values from -0.21875 to 0.21875
- lift_rows: float32 [16, 4, 2, 256, 256], P(('group', 'box'), 'freq', None, 'row'), parts along dimension 0, may hold values from -0.125 to 0.125
- probe_rows: float32 [16, 4, 2, 256, 256], P(('group', 'box'), 'freq', None, 'row'), parts along dimension 0, may hold values from -0.125 to 0.125
- wavenumber: float32 [8], P(('group', 'freq')), parts along dimension 0, may hold values from 0.7 to 1.4
- contrast: float32 [16, 256], P(('group', 'box'), 'row'), parts along dimension 0, may hold values from 0 to 1
- tree_order: int32 [16], P('group'), parts along dimension 0, may hold values from 0 to 7, each once
- illumination: float32 [2, 4, 2, 256, 32], P('group', 'freq'), parts along dimension 0, may hold values from -6 to 6
- observed: float32 [2, 4, 2, 256, 32], P('group', 'freq'), parts along dimension 0, may hold values from -3 to 3
Outputs:
- contrast_gradient: float32 [16, 256], P(('group', 'box'), 'row'), parts along dimension 0
The draws below stay inside these ranges and needn't reach their ends.
There are 2 independent parts, one for each index of `group`. The reference program is written for one: setup_inputs(seed, part) draws one part's arguments, and reference() takes and returns one part's arrays. A program takes and returns all parts, laid end to end along the dimension named above; each array names one. Nothing has to cross between parts.
Inputs may be any that keep to these rules, and one draw needn't show every extreme that they name: tree_order is a permutation of the 8 stored rows.
All inputs are finite; a program needn't handle non-finite values.
Results may differ from the reference program's by a relative error of at most 0.0003.
Values sent between devices are 32-bit elements; how exact they have to be, the bound alone decides.
A program may use at most 64 MiB of HBM per device.

```python
import math
from functools import partial
import jax
import jax.numpy as jnp
from jax import lax

M = 256
NPTS = 256
LEVELS = 3
NEWTON = 2
SOURCES = 32
FREQS = 4
LEAVES = 8
TOPS = 1


def block_levels(own_key, extent, split, smallest, high):
    level = 1.0
    for dim, shards_of in split:
        heights = jax.random.uniform(jax.random.fold_in(jax.random.fold_in(own_key, 6), dim), (shards_of,), jnp.float32, smallest / len(split), high / len(split))
        level = level * jnp.repeat(jnp.exp(heights), extent[dim] // shards_of).reshape((-1,) + (1,) * (len(extent) - 1 - dim))
    return level


def noise(own_key, shape, width, bound, pieces=(), held_as=jnp.bfloat16):
    array = jax.random.normal(own_key, shape, jnp.float32) * width
    if len(pieces) > 0:
        array = block_levels(own_key, shape, pieces, -0.22, 0.18) * array
    return jnp.clip(array, min=-bound, max=bound).astype(held_as)


def setup_inputs(seed: int = 0, part: int = 0) -> dict:
    key_of = jax.random.split(jax.random.key(seed), 9)
    own_keys = jax.random.split(jax.random.fold_in(key_of[8], part), 9)
    return {
        "base_maps": noise(own_keys[0], (LEAVES, FREQS, 2, M, M), (3 * M) ** -0.5, 0.21875, ((0, 4), (1, 2)), jnp.float32),
        "lift_rows": noise(own_keys[1], (LEAVES, FREQS, 2, NPTS, M), (8 * NPTS) ** -0.5, 0.125, ((0, 4), (1, 2), (3, 2)), jnp.float32),
        "probe_rows": noise(own_keys[2], (LEAVES, FREQS, 2, NPTS, M), (8 * M) ** -0.5, 0.125, ((0, 4), (1, 2), (3, 2)), jnp.float32),
        "wavenumber": jnp.clip(jnp.exp(math.log(1.4) - 0.6931472 * jax.random.uniform(own_keys[3], (FREQS,), jnp.float32) ** block_levels(own_keys[3], (FREQS,), ((0, 2),), -0.2, 0.2)), 0.7, 1.4),
        "contrast": jnp.clip(1.0 * jax.random.uniform(own_keys[4], (LEAVES, NPTS), jnp.float32) ** block_levels(own_keys[4], (LEAVES, NPTS), ((0, 4), (1, 2)), -0.2, 0.2), 0.0, 1.0),
        "tree_order": jax.random.permutation(own_keys[5], LEAVES).astype(jnp.int32),
        "illumination": noise(own_keys[6], (TOPS, FREQS, 2, M, SOURCES), 1.0, 6.0, ((1, 2),), jnp.float32),
        "observed": noise(own_keys[7], (TOPS, FREQS, 2, M, SOURCES), 0.5, 3.0, ((1, 2),), jnp.float32),
    }


def complex_mul(matrix_a, matrix_b):
    product = partial(jnp.matmul, precision=lax.Precision.HIGHEST)
    real_a, imag_a = matrix_a[..., 0, :, :], matrix_a[..., 1, :, :]
    real_b, imag_b = matrix_b[..., 0, :, :], matrix_b[..., 1, :, :]
    return jnp.stack([product(real_a, real_b) - product(imag_a, imag_b), product(real_a, imag_b) + product(imag_a, real_b)], axis=-3)


def conj_transpose(matrix):
    return jnp.stack([jnp.swapaxes(matrix[..., 0, :, :], -1, -2), -jnp.swapaxes(matrix[..., 1, :, :], -1, -2)], axis=-3)


def approx_inverse(coupled):
    real_part = coupled[..., 0, :, :]
    unit = jnp.broadcast_to(jnp.eye(coupled.shape[-1], dtype=coupled.dtype), real_part.shape)
    identity = jnp.stack([unit, jnp.zeros_like(real_part)], axis=-3)
    system = identity - coupled
    iterate = identity + coupled
    for sweep in range(NEWTON - 1):
        iterate = complex_mul(iterate, 2.0 * identity - complex_mul(system, iterate))
    return iterate


def split_blocks(matrix, half):
    return matrix[..., :half, :half], matrix[..., :half, half:], matrix[..., half:, :half], matrix[..., half:, half:]


def merge_pair(west, east):
    half = west.shape[-1] // 2
    west_outer, west_cross, west_enter, west_inner = split_blocks(west, half)
    east_outer, east_cross, east_enter, east_inner = split_blocks(east, half)
    forward_inv = approx_inverse(complex_mul(east_inner, west_inner))
    backward_inv = approx_inverse(complex_mul(west_inner, east_inner))
    reach_west = complex_mul(forward_inv, complex_mul(east_inner, west_enter))
    reach_east = complex_mul(forward_inv, east_enter)
    echo_west = west_enter + complex_mul(west_inner, reach_west)
    echo_east = complex_mul(west_inner, reach_east)
    top_rows = jnp.concatenate([west_outer + complex_mul(west_cross, reach_west), complex_mul(west_cross, reach_east)], axis=-1)
    bottom_rows = jnp.concatenate([complex_mul(east_cross, echo_west), east_outer + complex_mul(east_cross, echo_east)], axis=-1)
    return jnp.concatenate([top_rows, bottom_rows], axis=-2), forward_inv, backward_inv


def descend_pair(west, east, forward_inv, backward_inv, incoming, adjoint):
    half = west.shape[-1] // 2
    west_outer, west_cross, west_enter, west_inner = split_blocks(west, half)
    east_outer, east_cross, east_enter, east_inner = split_blocks(east, half)
    given_west, given_east = incoming[..., :half, :], incoming[..., half:, :]
    back_west, back_east = adjoint[..., :half, :], adjoint[..., half:, :]
    into_west = complex_mul(west_enter, given_west)
    west_in = complex_mul(forward_inv, complex_mul(east_inner, into_west) + complex_mul(east_enter, given_east))
    east_in = into_west + complex_mul(west_inner, west_in)
    crossed = complex_mul(conj_transpose(west_cross), back_west)
    west_back = complex_mul(conj_transpose(backward_inv), complex_mul(conj_transpose(east_inner), crossed) + complex_mul(conj_transpose(east_cross), back_east))
    east_back = crossed + complex_mul(conj_transpose(west_inner), west_back)
    west_side = (jnp.concatenate([given_west, west_in], axis=-2), jnp.concatenate([back_west, west_back], axis=-2))
    east_side = (jnp.concatenate([given_east, east_in], axis=-2), jnp.concatenate([back_east, east_back], axis=-2))
    return west_side, east_side


def alternate(west, east):
    stacked = jnp.stack([west, east], axis=1)
    return stacked.reshape((-1,) + west.shape[1:])


def reference(base_maps, lift_rows, probe_rows, wavenumber, contrast, tree_order, illumination, observed):
    tree_contrast = contrast[tree_order]
    squared = wavenumber * wavenumber
    weighted = tree_contrast[:, None, None, :, None] * probe_rows * squared[None, :, None, None, None]
    node_maps = base_maps + complex_mul(jnp.swapaxes(lift_rows, -1, -2), weighted)
    saved = []
    for level in range(LEVELS):
        former = node_maps[0::2]
        latter = node_maps[1::2]
        node_maps, forward_inv, backward_inv = merge_pair(former, latter)
        saved.append((former, latter, forward_inv, backward_inv))
    misfit = complex_mul(node_maps, illumination) - observed
    incoming, adjoint = illumination, misfit
    for former, latter, forward_inv, backward_inv in reversed(saved):
        west_side, east_side = descend_pair(former, latter, forward_inv, backward_inv, incoming, adjoint)
        incoming = alternate(west_side[0], east_side[0])
        adjoint = alternate(west_side[1], east_side[1])
    conj_adjoint = jnp.stack([adjoint[..., 0, :, :], -adjoint[..., 1, :, :]], axis=-3)
    lifted = complex_mul(lift_rows, conj_adjoint)
    probed = complex_mul(probe_rows, incoming)
    contrib = lifted[:, :, 0] * probed[:, :, 0] - lifted[:, :, 1] * probed[:, :, 1]
    tree_gradient = jnp.einsum("lfks,f->lk", contrib, squared, precision=lax.Precision.HIGHEST)
    return jnp.zeros(tree_gradient.shape, tree_gradient.dtype).at[tree_order].set(tree_gradient)
```

```python
from functools import partial

import jax
import jax.numpy as jnp
from jax import lax
from jax.experimental import pallas as pl
from jax.experimental.pallas import tpu as pltpu
from jax.sharding import PartitionSpec as P

LEVELS = 3


def from_partner(block, axis, apart):
    count = lax.axis_size(axis)
    route = []
    for low in range(count):
        high = low | 1 << apart
        if high != low and high < count:
            route += [(low, high), (high, low)]
    return lax.ppermute(block, axis, route)


def complex_mul(matrix_a, matrix_b):
    product = partial(jnp.matmul, precision=lax.Precision.HIGHEST)
    real_a, imag_a = (matrix_a[..., 0, :, :], matrix_a[..., 1, :, :])
    real_b, imag_b = (matrix_b[..., 0, :, :], matrix_b[..., 1, :, :])
    return jnp.stack(
        [
            product(real_a, real_b) - product(imag_a, imag_b),
            product(real_a, imag_b) + product(imag_a, real_b),
        ],
        axis=-3,
    )


def conj_transpose(matrix):
    return jnp.stack(
        [jnp.swapaxes(matrix[..., 0, :, :], -1, -2), -jnp.swapaxes(matrix[..., 1, :, :], -1, -2)],
        axis=-3,
    )


def approx_inverse(coupled):
    real_part = coupled[..., 0, :, :]
    unit = jnp.broadcast_to(jnp.eye(coupled.shape[-1], dtype=coupled.dtype), real_part.shape)
    identity = jnp.stack([unit, jnp.zeros_like(real_part)], axis=-3)
    system = identity - coupled
    iterate = identity + coupled
    iterate = complex_mul(iterate, 2.0 * identity - complex_mul(system, iterate))
    return iterate


def split_blocks(matrix, half):
    return (
        matrix[..., :half, :half],
        matrix[..., :half, half:],
        matrix[..., half:, :half],
        matrix[..., half:, half:],
    )


def merge_pair(west, east):
    half = west.shape[-1] // 2
    west_outer, west_cross, west_enter, west_inner = split_blocks(west, half)
    east_outer, east_cross, east_enter, east_inner = split_blocks(east, half)
    forward_inv = approx_inverse(complex_mul(east_inner, west_inner))
    backward_inv = approx_inverse(complex_mul(west_inner, east_inner))
    reach_west = complex_mul(forward_inv, complex_mul(east_inner, west_enter))
    reach_east = complex_mul(forward_inv, east_enter)
    echo_west = west_enter + complex_mul(west_inner, reach_west)
    echo_east = complex_mul(west_inner, reach_east)
    top_rows = jnp.concatenate(
        [west_outer + complex_mul(west_cross, reach_west), complex_mul(west_cross, reach_east)],
        axis=-1,
    )
    bottom_rows = jnp.concatenate(
        [complex_mul(east_cross, echo_west), east_outer + complex_mul(east_cross, echo_east)],
        axis=-1,
    )
    return (jnp.concatenate([top_rows, bottom_rows], axis=-2), forward_inv, backward_inv)


def descend_pair(west, east, forward_inv, backward_inv, incoming, adjoint):
    half = west.shape[-1] // 2
    west_outer, west_cross, west_enter, west_inner = split_blocks(west, half)
    east_outer, east_cross, east_enter, east_inner = split_blocks(east, half)
    given_west, given_east = (incoming[..., :half, :], incoming[..., half:, :])
    back_west, back_east = (adjoint[..., :half, :], adjoint[..., half:, :])
    into_west = complex_mul(west_enter, given_west)
    west_in = complex_mul(
        forward_inv, complex_mul(east_inner, into_west) + complex_mul(east_enter, given_east)
    )
    east_in = into_west + complex_mul(west_inner, west_in)
    crossed = complex_mul(conj_transpose(west_cross), back_west)
    west_back = complex_mul(
        conj_transpose(backward_inv),
        complex_mul(conj_transpose(east_inner), crossed)
        + complex_mul(conj_transpose(east_cross), back_east),
    )
    east_back = crossed + complex_mul(conj_transpose(west_inner), west_back)
    west_side = (
        jnp.concatenate([given_west, west_in], axis=-2),
        jnp.concatenate([back_west, west_back], axis=-2),
    )
    east_side = (
        jnp.concatenate([given_east, east_in], axis=-2),
        jnp.concatenate([back_east, east_back], axis=-2),
    )
    return (west_side, east_side)


def alternate(west, east):
    stacked = jnp.stack([west, east], axis=1)
    return stacked.reshape((-1,) + west.shape[1:])


def body(
    base_maps, lift_rows, probe_rows, wavenumber, contrast, tree_order, illumination, observed
):
    highest = lax.Precision.HIGHEST
    leaf_count = contrast.shape[0]
    tree_depth = leaf_count.bit_length() - 1
    box_index = lax.axis_index("box")
    positions = box_index * leaf_count + jnp.arange(leaf_count, dtype=jnp.int32)
    mine_order = jnp.take(tree_order, positions)
    every_contrast = lax.all_gather(contrast, "box", axis=0, tiled=True)
    selector = (
        mine_order[:, None] == jnp.arange(every_contrast.shape[0], dtype=jnp.int32)[None, :]
    ).astype(jnp.float32)
    tree_contrast = jnp.matmul(selector, every_contrast, precision=highest)
    squared = wavenumber * wavenumber
    weighted = (
        tree_contrast[:, None, None, :, None] * probe_rows * squared[None, :, None, None, None]
    )
    lift_swapped = jnp.swapaxes(lift_rows, -1, -2)
    node_maps = base_maps + lax.psum(complex_mul(lift_swapped, weighted), "row")
    saved = []
    whole_map = node_maps
    for level in range(LEVELS):
        if node_maps.shape[0] >= 2:
            former = node_maps[0::2]
            latter = node_maps[1::2]
            side_flag = None
        else:
            bit_index = level - tree_depth
            sibling = from_partner(node_maps, "box", bit_index)
            side_flag = box_index // 2**bit_index % 2
            former = jnp.where(side_flag == 0, node_maps, sibling)
            latter = jnp.where(side_flag == 0, sibling, node_maps)
        whole_map, forward_inv, backward_inv = merge_pair(former, latter)
        saved.append((former, latter, forward_inv, backward_inv, side_flag))
        node_maps = whole_map
    top_index = box_index * leaf_count // 8
    incoming = lax.dynamic_slice_in_dim(illumination, top_index, 1, 0)
    target = lax.dynamic_slice_in_dim(observed, top_index, 1, 0)
    adjoint = complex_mul(whole_map, incoming) - target
    for former, latter, forward_inv, backward_inv, side_flag in reversed(saved):
        west_side, east_side = descend_pair(
            former, latter, forward_inv, backward_inv, incoming, adjoint
        )
        if side_flag is None:
            incoming = alternate(west_side[0], east_side[0])
            adjoint = alternate(west_side[1], east_side[1])
        else:
            incoming = jnp.where(side_flag == 0, west_side[0], east_side[0])
            adjoint = jnp.where(side_flag == 0, west_side[1], east_side[1])
    conj_adjoint = jnp.stack([adjoint[..., 0, :, :], -adjoint[..., 1, :, :]], axis=-3)
    lifted = complex_mul(lift_rows, conj_adjoint)
    probed = complex_mul(probe_rows, incoming)
    contrib = lifted[:, :, 0] * probed[:, :, 0] - lifted[:, :, 1] * probed[:, :, 1]
    partial_grad = jnp.einsum("lfks,f->lk", contrib, squared, precision=highest)
    total = lax.psum(partial_grad, "freq")
    rows_here = jnp.arange(lax.axis_size("box") * leaf_count, dtype=jnp.int32)
    chooser = (rows_here[:, None] == mine_order[None, :]).astype(jnp.float32)
    return lax.psum_scatter(
        jnp.matmul(chooser, total, precision=highest), "box", scatter_dimension=0, tiled=True
    )


H = 128
MESH = pl.DeviceIdType.MESH
F32 = jnp.float32


def halves(x):
    high = x.astype(jnp.bfloat16)
    return high, (x - high.astype(F32)).astype(jnp.bfloat16)


def mm(a, b):
    dot = partial(jnp.dot, preferred_element_type=F32)
    return dot(a[0], b[0]) + (dot(a[0], b[1]) + dot(a[1], b[0]))


def blk(x):
    turned = jnp.concatenate([-x[H:], x[:H]], axis=0)
    return jnp.concatenate([x, turned], axis=1)


def apply_iterate(op, x):
    once = mm(op, halves(x))
    even = x + mm(op, halves(once))
    return even + mm(op, halves(even))


def pack(x):
    q = x.shape[0] // 4
    return jnp.concatenate([x[i * q : (i + 1) * q] for i in range(4)], axis=1)


def unpack(x):
    q = x.shape[1] // 4
    return jnp.concatenate([x[:, i * q : (i + 1) * q] for i in range(4)], axis=0)


def adjoint_maps(a13, a33, b23, b33):
    op_a33, op_a13, op_b23 = halves(blk(a33)), halves(blk(a13)), halves(blk(b23))
    split_b33, split_a33 = halves(b33), halves(a33)
    coupled = mm(op_a33, split_b33)
    op = halves(blk(coupled))
    row = lax.broadcasted_iota(jnp.int32, (2 * H, H), 0)
    col = lax.broadcasted_iota(jnp.int32, (2 * H, H), 1)
    even = jnp.where(row == col, 1.0, 0.0) + mm(op, halves(coupled))
    inverse = halves(even + mm(op, halves(even)))
    f1 = blk(mm(halves(blk(mm(op_a13, split_b33))), inverse))
    f2 = blk(mm(op_b23, inverse))
    g1 = blk(a13 + mm(halves(f1), split_a33))
    g2 = blk(mm(halves(f2), split_a33))
    to_l3 = jnp.concatenate([f1.T, f2.T], axis=1)
    to_k3 = jnp.concatenate([g1.T, g2.T], axis=1)
    return to_l3, to_k3


def incoming_maps(op_a33, op, b33a31, a31, b32):
    reach = apply_iterate(op, jnp.concatenate([b33a31, b32], axis=1))
    echo = mm(op_a33, halves(reach))
    return reach, jnp.concatenate([echo[:, :H] + a31, echo[:, H:]], axis=1)


def wide(x):
    return jnp.concatenate([blk(x[:, :H]), blk(x[:, H:])], axis=1)


def store_halves(ref, x):
    high, low = halves(x)
    ref[0] = high
    ref[1] = low


def load_halves(ref):
    return ref[0], ref[1]


def kernel(
    base, lift, probe, wave, contrast, order, illum, observed, out,
    lbuf, pbuf, bbuf, cbuf, own, got, t33, tvec, mbuf, vbuf, inc1, adj1, inc2, adj2,
    gpart, grecv, gtot, loc_sem, xs_sem, xr_sem, cs_sem, cr_sem, zs_sem, zr_sem,
    ts_sem, tr_sem, us_sem, ur_sem, ms_sem, mr_sem, vs_sem, vr_sem, gs_sem, gr_sem, hs_sem, hr_sem,
):
    box = lax.axis_index("box")
    row = lax.axis_index("row")
    core = lax.axis_index("freq")
    side = lax.rem(box, 2)
    pair = box // 2
    mate = box + 1 - 2 * side
    other = 1 - row
    boxes = [lax.rem(box + d, 4) for d in (1, 2, 3)]
    peers = [{"row": other, "freq": core}, {"row": row, "freq": 1 - core}, {"row": other, "freq": 1 - core}]

    def remote(source, target, sender, receiver, where):
        return pltpu.make_async_remote_copy(
            src_ref=source, dst_ref=target, send_sem=sender, recv_sem=receiver,
            device_id=where, device_id_type=MESH,
        )

    mine = pl.ds(pl.multiple_of(row * H, H), H)
    theirs = pl.ds(pl.multiple_of(other * H, H), H)
    loads = []
    for leaf in range(2):
        loads += [
            (lift.at[leaf, row], lbuf.at[leaf, :, mine, :]),
            (probe.at[leaf, row], pbuf.at[leaf, :, mine, :]),
            (base.at[leaf, row], bbuf.at[leaf]),
        ]
    loads = [pltpu.make_async_copy(s, t, loc_sem.at[i]) for i, (s, t) in enumerate(loads)]
    for load in loads:
        load.start()

    barrier = pltpu.get_barrier_semaphore()
    for where in peers + [{"box": b} for b in boxes]:
        pl.semaphore_signal(barrier, inc=1, device_id=where, device_id_type=MESH)
    pl.semaphore_wait(barrier, 6)

    cbuf[box, row] = contrast[...]
    ahead = remote(contrast, cbuf.at[box, row], xs_sem.at[8], xr_sem.at[8], peers[0])
    ahead.start()
    low, high = pl.ds(0, H), pl.ds(H, H)
    plan = [(lift, lbuf, 0, high), (probe, pbuf, 0, high), (lift, lbuf, 1, high), (probe, pbuf, 1, high)]
    plan += [(probe, pbuf, 0, low), (probe, pbuf, 1, low), (lift, lbuf, 0, low), (lift, lbuf, 1, low)]
    sends, waits = [ahead], []
    for i, (source, target, leaf, cols) in enumerate(plan):
        copy = remote(
            source.at[leaf, other, :, :, cols], target.at[leaf, :, mine, cols],
            xs_sem.at[i], xr_sem.at[i], peers[0],
        )
        copy.start()
        sends.append(copy)
        waits.append(
            remote(
                source.at[leaf, other, :, :, cols], target.at[leaf, :, theirs, cols],
                xs_sem.at[i], xr_sem.at[i], peers[0],
            )
        )

    remote(contrast, cbuf.at[box, other], xs_sem.at[8], xr_sem.at[8], peers[0]).wait_recv()
    for d in range(3):
        copy = remote(cbuf.at[box], cbuf.at[box], cs_sem.at[d], cr_sem.at[box], {"box": boxes[d]})
        copy.start()
        sends.append(copy)
    for d in range(3):
        slot = cbuf.at[boxes[d]]
        remote(slot, slot, cs_sem.at[d], cr_sem.at[boxes[d]], {"box": boxes[d]}).wait_recv()
    number = wave[row]
    squared = number * number
    weight = []
    for leaf in range(2):
        stored = order[box * 2 + leaf]
        total = jnp.zeros((2, H), F32)
        for j in range(8):
            total = total + jnp.where(stored == j, cbuf[j // 2, :, j % 2, :], 0.0)
        total = total * squared
        weight.append(
            jnp.concatenate([jnp.broadcast_to(total[i : i + 1], (H, H)).T for i in range(2)], axis=0)
        )

    for load in loads:
        load.wait()
    for copy in waits[:4]:
        copy.wait_recv()

    def lift_op(leaf, cols):
        real, imag = lbuf[leaf, 0, :, cols].T, lbuf[leaf, 1, :, cols].T
        upper = jnp.concatenate([real, -imag], axis=1)
        return halves(jnp.concatenate([upper, jnp.concatenate([imag, real], axis=1)], axis=0))

    def weighted(leaf, cols):
        both = [pbuf[leaf, part, :, cols] * weight[leaf] for part in range(2)]
        return halves(jnp.concatenate(both, axis=0))

    def based(leaf, rows, cols):
        return jnp.concatenate([bbuf[leaf, 0, rows, cols], bbuf[leaf, 1, rows, cols]], axis=0)

    op3 = [lift_op(leaf, high) for leaf in range(2)]
    w3 = [weighted(leaf, high) for leaf in range(2)]
    a33, b33 = [based(leaf, high, high) + mm(op3[leaf], w3[leaf]) for leaf in range(2)]
    op_a33, op_b33 = halves(blk(a33)), halves(blk(b33))
    op = halves(blk(mm(op_b33, halves(a33))))
    for copy in waits[4:6]:
        copy.wait_recv()
    w1 = [weighted(leaf, low) for leaf in range(2)]
    a31, b32 = [based(leaf, high, low) + mm(op3[leaf], w1[leaf]) for leaf in range(2)]
    reach, echo = incoming_maps(op_a33, op, mm(op_b33, halves(a31)), a31, b32)
    for copy in waits[6:]:
        copy.wait_recv()
    op1 = [lift_op(leaf, low) for leaf in range(2)]
    a13, b23 = [based(leaf, low, high) + mm(op1[leaf], w3[leaf]) for leaf in range(2)]
    a11, b22 = [based(leaf, low, low) + mm(op1[leaf], w1[leaf]) for leaf in range(2)]
    bottom = mm(halves(blk(b23)), halves(echo))
    top = mm(halves(blk(a13)), halves(reach))
    top_left, top_right = top[:, :H] + a11, top[:, H:]
    low_left, low_right = bottom[:, :H], bottom[:, H:] + b22
    own[0] = low_right
    own[1] = low_left
    own[2] = top_right
    for i in range(3):
        copy = remote(own.at[i], got.at[i], zs_sem.at[i], zr_sem.at[i], {"box": mate})
        copy.start()
        sends.append(copy)
    store_halves(inc1.at[0], wide(reach))
    store_halves(inc1.at[1], wide(echo))
    to_l3, to_k3 = adjoint_maps(a13, a33, b23, b33)
    store_halves(adj1.at[0], to_l3)
    store_halves(adj1.at[1], to_k3)

    def illum_half(ref, part):
        rows = pl.ds(part * H, H)
        return jnp.concatenate([ref[0, row, 0, rows, :], ref[0, row, 1, rows, :]], axis=0)

    i1, j2 = illum_half(illum, 0), illum_half(illum, 1)
    upper_pair = pair == 1
    east = side == 1
    given = jnp.where(upper_pair, j2, i1)

    for i in range(2):
        remote(own.at[i], got.at[i], zs_sem.at[i], zr_sem.at[i], {"box": mate}).wait_recv()
    a33, b33 = jnp.where(east, got[0], low_right), jnp.where(east, low_right, got[0])
    a31, b32 = jnp.where(east, got[1], low_left), jnp.where(east, low_left, got[1])
    op_a33, op_b33 = halves(blk(a33)), halves(blk(b33))
    op = halves(blk(mm(op_b33, halves(a33))))
    reach, echo = incoming_maps(op_a33, op, mm(op_b33, halves(a31)), a31, b32)
    half_map = mm(halves(blk(top_right)), halves(jnp.where(east, echo, reach)))
    left = half_map[:, :H] + jnp.where(east, 0.0, top_left)
    right = half_map[:, H:] + jnp.where(east, top_left, 0.0)
    op_left, op_right = halves(blk(left)), halves(blk(right))

    @pl.when(east)
    def _():
        t33[pair] = right
        tvec[pair] = pack(mm(op_left, halves(given)))
        for d in range(3):
            where = {"box": boxes[d]}
            remote(t33.at[pair], t33.at[pair], ts_sem.at[d], tr_sem.at[pair], where).start()
            remote(tvec.at[pair], tvec.at[pair], us_sem.at[d], ur_sem.at[pair], where).start()

    store_halves(inc2, wide(jnp.where(east, echo, reach)))
    remote(own.at[2], got.at[2], zs_sem.at[2], zr_sem.at[2], {"box": mate}).wait_recv()
    a13, b23 = jnp.where(east, got[2], top_right), jnp.where(east, top_right, got[2])
    to_l3, to_k3 = adjoint_maps(a13, a33, b23, b33)
    store_halves(adj2, jnp.where(east, to_k3, to_l3))
    op_right_t = halves(blk(right).T)

    for s in range(2):

        @pl.when(box != 2 * s + 1)
        def _():
            where = {"box": boxes[0]}
            remote(t33.at[s], t33.at[s], ts_sem.at[0], tr_sem.at[s], where).wait_recv()
            remote(tvec.at[s], tvec.at[s], us_sem.at[0], ur_sem.at[s], where).wait_recv()

    a33, b33 = t33[0], t33[1]
    enter = unpack(tvec[0])
    full_a33, full_b33 = blk(a33), blk(b33)
    op_a33, op_b33 = halves(full_a33), halves(full_b33)
    op = halves(blk(mm(op_b33, halves(a33))))
    i3 = apply_iterate(op, mm(op_b33, halves(enter)) + unpack(tvec[1]))
    j3 = enter + mm(op_a33, halves(i3))
    inner = jnp.where(upper_pair, j3, i3)

    @pl.when(side == 0)
    def _():
        goal = jnp.where(upper_pair, illum_half(observed, 1), illum_half(observed, 0))
        misfit = mm(op_left, halves(given)) + mm(op_right, halves(inner)) - goal
        mbuf[...] = pack(misfit)
        vbuf[pair] = pack(mm(op_right_t, halves(misfit)))
        for d in range(3):
            remote(vbuf.at[pair], vbuf.at[pair], vs_sem.at[d], vr_sem.at[pair], {"box": boxes[d]}).start()
        remote(mbuf, mbuf, ms_sem, mr_sem, {"box": mate}).start()

    flip_a33, flip_b33 = full_a33.T, full_b33.T
    op_at, op_bt = halves(flip_a33), halves(flip_b33)
    op = halves(blk(mm(op_bt, halves(flip_a33[:, :H]))))

    for s in range(2):

        @pl.when(box != 2 * s)
        def _():
            remote(vbuf.at[s], vbuf.at[s], vs_sem.at[0], vr_sem.at[s], {"box": boxes[0]}).wait_recv()

    crossed = unpack(vbuf[0])
    l3 = apply_iterate(op, mm(op_bt, halves(crossed)) + unpack(vbuf[1]))
    k3 = crossed + mm(op_at, halves(l3))

    @pl.when(east)
    def _():
        remote(mbuf, mbuf, ms_sem, mr_sem, {"box": mate}).wait_recv()

    back = unpack(mbuf[...])
    below = jnp.where(upper_pair, k3, l3)
    inner_in = mm(load_halves(inc2), halves(jnp.concatenate([given, inner], axis=0)))
    inner_back = mm(load_halves(adj2), halves(jnp.concatenate([back, below], axis=0)))
    in_outer = jnp.where(east, inner, given)
    back_outer = jnp.where(east, below, back)
    split_in = halves(jnp.concatenate([in_outer, inner_in], axis=0))
    split_back = halves(jnp.concatenate([back_outer, inner_back], axis=0))

    ones = jnp.ones((8, 32), jnp.bfloat16)
    across = (((1,), (1,)), ((), ()))
    for leaf in range(2):
        outer_in = inner_in if leaf else in_outer
        outer_back = inner_back if leaf else back_outer
        leaf_in = mm(load_halves(inc1.at[leaf]), split_in)
        leaf_back = mm(load_halves(adj1.at[leaf]), split_back)
        in_re = jnp.concatenate([outer_in[:H], leaf_in[:H]], axis=0)
        in_im = jnp.concatenate([outer_in[H:], leaf_in[H:]], axis=0)
        back_re = jnp.concatenate([outer_back[:H], leaf_back[:H]], axis=0)
        back_im = jnp.concatenate([outer_back[H:], leaf_back[H:]], axis=0)
        probe_in = jnp.concatenate(
            [jnp.concatenate([in_re, in_im], axis=1), jnp.concatenate([-in_im, in_re], axis=1)], axis=0
        )
        lift_in = jnp.concatenate(
            [jnp.concatenate([back_re, -back_im], axis=1), jnp.concatenate([back_im, back_re], axis=1)], axis=0
        )
        lifted = mm(halves(jnp.concatenate([lbuf[leaf, 0], lbuf[leaf, 1]], axis=1)), halves(lift_in))
        probed = mm(halves(jnp.concatenate([pbuf[leaf, 0], pbuf[leaf, 1]], axis=1)), halves(probe_in))
        contrib = lifted[:, :32] * probed[:, :32] - lifted[:, 32:] * probed[:, 32:]
        contrib = halves(contrib * squared)
        summed = [lax.dot_general(ones, part, across, preferred_element_type=F32) for part in contrib]
        summed = summed[0] + summed[1]
        gpart[0, leaf : leaf + 1, :] = summed[0:1, :H]
        gpart[1, leaf : leaf + 1, :] = summed[0:1, H:]

    place = row * 2 + core
    grecv[place] = gpart[row]
    ends = []
    for d, (r, c) in enumerate([(other, core), (row, 1 - core), (other, 1 - core)]):
        copy = remote(gpart.at[r], grecv.at[place], gs_sem.at[d], gr_sem.at[place], peers[d])
        copy.start()
        sends.append(copy)
        slot = grecv.at[r * 2 + c]
        ends.append(remote(slot, slot, gs_sem.at[d], gr_sem.at[r * 2 + c], peers[d]))
    for copy in ends:
        copy.wait_recv()
    gtot[box] = (grecv[0] + grecv[1]) + (grecv[2] + grecv[3])
    for d in range(3):
        copy = remote(gtot.at[box], gtot.at[box], hs_sem.at[d], hr_sem.at[box], {"box": boxes[d]})
        copy.start()
        sends.append(copy)
    for d in range(3):
        slot = gtot.at[boxes[d]]
        remote(slot, slot, hs_sem.at[d], hr_sem.at[boxes[d]], {"box": boxes[d]}).wait_recv()
    for j in range(2):
        total = jnp.zeros((1, H), F32)
        for t in range(8):
            total = total + jnp.where(order[t] == box * 2 + j, gtot[t // 2, t % 2 : t % 2 + 1, :], 0.0)
        out[j : j + 1, :] = total

    for copy in sends:
        copy.wait_send()

    @pl.when(east)
    def _():
        for d in range(3):
            where = {"box": boxes[d]}
            remote(t33.at[pair], t33.at[pair], ts_sem.at[d], tr_sem.at[pair], where).wait_send()
            remote(tvec.at[pair], tvec.at[pair], us_sem.at[d], ur_sem.at[pair], where).wait_send()

    @pl.when(side == 0)
    def _():
        for d in range(3):
            remote(vbuf.at[pair], vbuf.at[pair], vs_sem.at[d], vr_sem.at[pair], {"box": boxes[d]}).wait_send()
        remote(mbuf, mbuf, ms_sem, mr_sem, {"box": mate}).wait_send()


def fused(*args):
    half = jnp.bfloat16
    dma = pltpu.SemaphoreType.DMA
    scratch = [
        pltpu.VMEM((2, 2, 2 * H, 2 * H), F32),
        pltpu.VMEM((2, 2, 2 * H, 2 * H), F32),
        pltpu.VMEM((2, 2, 2 * H, 2 * H), F32),
        pltpu.VMEM((4, 2, 2, H), F32),
        pltpu.VMEM((3, 2 * H, H), F32),
        pltpu.VMEM((3, 2 * H, H), F32),
        pltpu.VMEM((2, 2 * H, H), F32),
        pltpu.VMEM((2, H // 2, H), F32),
        pltpu.VMEM((H // 2, H), F32),
        pltpu.VMEM((2, H // 2, H), F32),
        pltpu.VMEM((2, 2, 2 * H, 4 * H), half),
        pltpu.VMEM((2, 2, 2 * H, 4 * H), half),
        pltpu.VMEM((2, 2 * H, 4 * H), half),
        pltpu.VMEM((2, 2 * H, 4 * H), half),
        pltpu.VMEM((2, 2, H), F32),
        pltpu.VMEM((4, 2, H), F32),
        pltpu.VMEM((4, 2, H), F32),
        dma((6,)), dma((9,)), dma((9,)), dma((3,)), dma((4,)), dma((3,)), dma((3,)),
        dma((3,)), dma((2,)), dma((3,)), dma((2,)), dma(()), dma(()), dma((3,)), dma((2,)),
        dma((3,)), dma((4,)), dma((3,)), dma((4,)),
    ]
    hbm, vmem, smem = [
        pl.BlockSpec(memory_space=space) for space in (pl.ANY, pltpu.VMEM, pltpu.SMEM)
    ]
    return pl.pallas_call(
        kernel,
        out_shape=jax.ShapeDtypeStruct((2, H), F32),
        in_specs=[hbm, hbm, hbm, smem, vmem, smem, vmem, vmem],
        out_specs=vmem,
        scratch_shapes=scratch,
        compiler_params=pltpu.CompilerParams(
            collective_id=0, has_side_effects=True, vmem_limit_bytes=48 * 2**20
        ),
        name="gradient",
    )(*args)


def pick(mesh):
    def local(*args):
        shape = mesh.shape
        fits = shape["box"] == 4 and shape["row"] == 2 and shape["freq"] == 2
        fits = fits and args[0].shape == (2, 2, 2, 256, 256) and args[6].shape == (1, 2, 2, 256, 32)
        return (fused if fits else body)(*args)

    return local


def solution(mesh):
    return jax.shard_map(
        pick(mesh),
        mesh=mesh,
        in_specs=(
            P(("group", "box"), "freq", None, None, None),
            P(("group", "box"), "freq", None, "row", None),
            P(("group", "box"), "freq", None, "row", None),
            P(("group", "freq")),
            P(("group", "box"), "row"),
            P("group"),
            P("group", "freq", None, None, None),
            P("group", "freq", None, None, None),
        ),
        out_specs=P(("group", "box"), "row"),
        check_vma=False,
    )
```

```python
from functools import partial

import jax
import jax.numpy as jnp
from jax import lax
from jax.experimental import pallas as pl
from jax.experimental.pallas import tpu as pltpu
from jax.sharding import PartitionSpec as P

LEVELS = 3


def from_partner(block, axis, apart):
    count = lax.axis_size(axis)
    route = []
    for low in range(count):
        high = low | 1 << apart
        if high != low and high < count:
            route += [(low, high), (high, low)]
    return lax.ppermute(block, axis, route)


def complex_mul(matrix_a, matrix_b):
    product = partial(jnp.matmul, precision=lax.Precision.HIGHEST)
    real_a, imag_a = (matrix_a[..., 0, :, :], matrix_a[..., 1, :, :])
    real_b, imag_b = (matrix_b[..., 0, :, :], matrix_b[..., 1, :, :])
    return jnp.stack(
        [
            product(real_a, real_b) - product(imag_a, imag_b),
            product(real_a, imag_b) + product(imag_a, real_b),
        ],
        axis=-3,
    )


def conj_transpose(matrix):
    return jnp.stack(
        [jnp.swapaxes(matrix[..., 0, :, :], -1, -2), -jnp.swapaxes(matrix[..., 1, :, :], -1, -2)],
        axis=-3,
    )


def approx_inverse(coupled):
    real_part = coupled[..., 0, :, :]
    unit = jnp.broadcast_to(jnp.eye(coupled.shape[-1], dtype=coupled.dtype), real_part.shape)
    identity = jnp.stack([unit, jnp.zeros_like(real_part)], axis=-3)
    system = identity - coupled
    iterate = identity + coupled
    iterate = complex_mul(iterate, 2.0 * identity - complex_mul(system, iterate))
    return iterate


def split_blocks(matrix, half):
    return (
        matrix[..., :half, :half],
        matrix[..., :half, half:],
        matrix[..., half:, :half],
        matrix[..., half:, half:],
    )


def merge_pair(west, east):
    half = west.shape[-1] // 2
    west_outer, west_cross, west_enter, west_inner = split_blocks(west, half)
    east_outer, east_cross, east_enter, east_inner = split_blocks(east, half)
    forward_inv = approx_inverse(complex_mul(east_inner, west_inner))
    backward_inv = approx_inverse(complex_mul(west_inner, east_inner))
    reach_west = complex_mul(forward_inv, complex_mul(east_inner, west_enter))
    reach_east = complex_mul(forward_inv, east_enter)
    echo_west = west_enter + complex_mul(west_inner, reach_west)
    echo_east = complex_mul(west_inner, reach_east)
    top_rows = jnp.concatenate(
        [west_outer + complex_mul(west_cross, reach_west), complex_mul(west_cross, reach_east)],
        axis=-1,
    )
    bottom_rows = jnp.concatenate(
        [complex_mul(east_cross, echo_west), east_outer + complex_mul(east_cross, echo_east)],
        axis=-1,
    )
    return (jnp.concatenate([top_rows, bottom_rows], axis=-2), forward_inv, backward_inv)


def descend_pair(west, east, forward_inv, backward_inv, incoming, adjoint):
    half = west.shape[-1] // 2
    west_outer, west_cross, west_enter, west_inner = split_blocks(west, half)
    east_outer, east_cross, east_enter, east_inner = split_blocks(east, half)
    given_west, given_east = (incoming[..., :half, :], incoming[..., half:, :])
    back_west, back_east = (adjoint[..., :half, :], adjoint[..., half:, :])
    into_west = complex_mul(west_enter, given_west)
    west_in = complex_mul(
        forward_inv, complex_mul(east_inner, into_west) + complex_mul(east_enter, given_east)
    )
    east_in = into_west + complex_mul(west_inner, west_in)
    crossed = complex_mul(conj_transpose(west_cross), back_west)
    west_back = complex_mul(
        conj_transpose(backward_inv),
        complex_mul(conj_transpose(east_inner), crossed)
        + complex_mul(conj_transpose(east_cross), back_east),
    )
    east_back = crossed + complex_mul(conj_transpose(west_inner), west_back)
    west_side = (
        jnp.concatenate([given_west, west_in], axis=-2),
        jnp.concatenate([back_west, west_back], axis=-2),
    )
    east_side = (
        jnp.concatenate([given_east, east_in], axis=-2),
        jnp.concatenate([back_east, east_back], axis=-2),
    )
    return (west_side, east_side)


def alternate(west, east):
    stacked = jnp.stack([west, east], axis=1)
    return stacked.reshape((-1,) + west.shape[1:])


def body(
    base_maps, lift_rows, probe_rows, wavenumber, contrast, tree_order, illumination, observed
):
    highest = lax.Precision.HIGHEST
    leaf_count = contrast.shape[0]
    tree_depth = leaf_count.bit_length() - 1
    box_index = lax.axis_index("box")
    positions = box_index * leaf_count + jnp.arange(leaf_count, dtype=jnp.int32)
    mine_order = jnp.take(tree_order, positions)
    every_contrast = lax.all_gather(contrast, "box", axis=0, tiled=True)
    selector = (
        mine_order[:, None] == jnp.arange(every_contrast.shape[0], dtype=jnp.int32)[None, :]
    ).astype(jnp.float32)
    tree_contrast = jnp.matmul(selector, every_contrast, precision=highest)
    squared = wavenumber * wavenumber
    weighted = (
        tree_contrast[:, None, None, :, None] * probe_rows * squared[None, :, None, None, None]
    )
    lift_swapped = jnp.swapaxes(lift_rows, -1, -2)
    node_maps = base_maps + lax.psum(complex_mul(lift_swapped, weighted), "row")
    saved = []
    whole_map = node_maps
    for level in range(LEVELS):
        if node_maps.shape[0] >= 2:
            former = node_maps[0::2]
            latter = node_maps[1::2]
            side_flag = None
        else:
            bit_index = level - tree_depth
            sibling = from_partner(node_maps, "box", bit_index)
            side_flag = box_index // 2**bit_index % 2
            former = jnp.where(side_flag == 0, node_maps, sibling)
            latter = jnp.where(side_flag == 0, sibling, node_maps)
        whole_map, forward_inv, backward_inv = merge_pair(former, latter)
        saved.append((former, latter, forward_inv, backward_inv, side_flag))
        node_maps = whole_map
    top_index = box_index * leaf_count // 8
    incoming = lax.dynamic_slice_in_dim(illumination, top_index, 1, 0)
    target = lax.dynamic_slice_in_dim(observed, top_index, 1, 0)
    adjoint = complex_mul(whole_map, incoming) - target
    for former, latter, forward_inv, backward_inv, side_flag in reversed(saved):
        west_side, east_side = descend_pair(
            former, latter, forward_inv, backward_inv, incoming, adjoint
        )
        if side_flag is None:
            incoming = alternate(west_side[0], east_side[0])
            adjoint = alternate(west_side[1], east_side[1])
        else:
            incoming = jnp.where(side_flag == 0, west_side[0], east_side[0])
            adjoint = jnp.where(side_flag == 0, west_side[1], east_side[1])
    conj_adjoint = jnp.stack([adjoint[..., 0, :, :], -adjoint[..., 1, :, :]], axis=-3)
    lifted = complex_mul(lift_rows, conj_adjoint)
    probed = complex_mul(probe_rows, incoming)
    contrib = lifted[:, :, 0] * probed[:, :, 0] - lifted[:, :, 1] * probed[:, :, 1]
    partial_grad = jnp.einsum("lfks,f->lk", contrib, squared, precision=highest)
    total = lax.psum(partial_grad, "freq")
    rows_here = jnp.arange(lax.axis_size("box") * leaf_count, dtype=jnp.int32)
    chooser = (rows_here[:, None] == mine_order[None, :]).astype(jnp.float32)
    return lax.psum_scatter(
        jnp.matmul(chooser, total, precision=highest), "box", scatter_dimension=0, tiled=True
    )


H = 128
MESH = pl.DeviceIdType.MESH
F32 = jnp.float32


def halves(x):
    high = x.astype(jnp.bfloat16)
    return high, (x - high.astype(F32)).astype(jnp.bfloat16)


def mm(a, b):
    dot = partial(jnp.dot, preferred_element_type=F32)
    return dot(a[0], b[0]) + (dot(a[0], b[1]) + dot(a[1], b[0]))


def blk(x):
    turned = jnp.concatenate([-x[H:], x[:H]], axis=0)
    return jnp.concatenate([x, turned], axis=1)


def apply_iterate(op, x):
    once = mm(op, halves(x))
    even = x + mm(op, halves(once))
    return even + mm(op, halves(even))


def pack(x):
    q = x.shape[0] // 4
    return jnp.concatenate([x[i * q : (i + 1) * q] for i in range(4)], axis=1)


def unpack(x):
    q = x.shape[1] // 4
    return jnp.concatenate([x[:, i * q : (i + 1) * q] for i in range(4)], axis=0)


def adjoint_maps(a13, a33, b23, b33):
    op_a33, op_a13, op_b23 = halves(blk(a33)), halves(blk(a13)), halves(blk(b23))
    split_b33, split_a33 = halves(b33), halves(a33)
    coupled = mm(op_a33, split_b33)
    op = halves(blk(coupled))
    row = lax.broadcasted_iota(jnp.int32, (2 * H, H), 0)
    col = lax.broadcasted_iota(jnp.int32, (2 * H, H), 1)
    even = jnp.where(row == col, 1.0, 0.0) + mm(op, halves(coupled))
    inverse = halves(even + mm(op, halves(even)))
    f1 = blk(mm(halves(blk(mm(op_a13, split_b33))), inverse))
    f2 = blk(mm(op_b23, inverse))
    g1 = blk(a13 + mm(halves(f1), split_a33))
    g2 = blk(mm(halves(f2), split_a33))
    to_l3 = jnp.concatenate([f1.T, f2.T], axis=1)
    to_k3 = jnp.concatenate([g1.T, g2.T], axis=1)
    return to_l3, to_k3


def incoming_maps(op_a33, op, b33a31, a31, b32):
    reach = apply_iterate(op, jnp.concatenate([b33a31, b32], axis=1))
    echo = mm(op_a33, halves(reach))
    return reach, jnp.concatenate([echo[:, :H] + a31, echo[:, H:]], axis=1)


def wide(x):
    return jnp.concatenate([blk(x[:, :H]), blk(x[:, H:])], axis=1)


def store_halves(ref, x):
    high, low = halves(x)
    ref[0] = high
    ref[1] = low


def load_halves(ref):
    return ref[0], ref[1]


def kernel(
    base, lift, probe, wave_in, contrast, order_in, illum_in, observed_in, out,
    wave, order, illum, observed, opl, opr, oprt, evec, gvec, es_sem, er_sem,
    lbuf, pbuf, bbuf, cbuf, own, got, t33, tvec, mbuf, vbuf, inc1, adj1, inc2, adj2,
    gpart, grecv, gtot, loc_sem, xs_sem, xr_sem, cs_sem, cr_sem, zs_sem, zr_sem,
    ts_sem, tr_sem, us_sem, ur_sem, ms_sem, mr_sem, vs_sem, vr_sem, gs_sem, gr_sem, hs_sem, hr_sem,
):
    box = lax.axis_index("box")
    row = lax.axis_index("row")
    core = lax.axis_index("freq")
    side = lax.rem(box, 2)
    pair = box // 2
    mate = box + 1 - 2 * side
    other = 1 - row
    boxes = [lax.rem(box + d, 4) for d in (1, 2, 3)]
    peers = [{"row": other, "freq": core}, {"row": row, "freq": 1 - core}, {"row": other, "freq": 1 - core}]

    def remote(source, target, sender, receiver, where):
        return pltpu.make_async_remote_copy(
            src_ref=source, dst_ref=target, send_sem=sender, recv_sem=receiver,
            device_id=where, device_id_type=MESH,
        )

    mine = pl.ds(pl.multiple_of(row * H, H), H)
    theirs = pl.ds(pl.multiple_of(other * H, H), H)
    loads = []
    for leaf in range(2):
        loads += [
            (lift.at[leaf, row], lbuf.at[leaf, :, mine, :]),
            (probe.at[leaf, row], pbuf.at[leaf, :, mine, :]),
            (base.at[leaf, row], bbuf.at[leaf]),
        ]
    loads += [(wave_in, wave), (order_in, order), (illum_in.at[0, row], illum)]
    loads += [(observed_in.at[0, row], observed), (contrast, cbuf.at[box, row])]
    loads = [pltpu.make_async_copy(s, t, loc_sem.at[i]) for i, (s, t) in enumerate(loads)]
    for load in loads:
        load.start()

    barrier = pltpu.get_barrier_semaphore()
    for where in peers + [{"box": b} for b in boxes]:
        pl.semaphore_signal(barrier, inc=1, device_id=where, device_id_type=MESH)
    pl.semaphore_wait(barrier, 6)

    early = remote(contrast, cbuf.at[box, row], xs_sem.at[8], xr_sem.at[8], peers[0])
    early.start()
    low, high = pl.ds(0, H), pl.ds(H, H)
    plan = [(lift, lbuf, 0, high), (probe, pbuf, 0, high), (lift, lbuf, 1, high), (probe, pbuf, 1, high)]
    plan += [(probe, pbuf, 0, low), (probe, pbuf, 1, low), (lift, lbuf, 0, low), (lift, lbuf, 1, low)]
    sends, waits = [early], []
    for i, (source, target, leaf, cols) in enumerate(plan):
        copy = remote(
            source.at[leaf, other, :, :, cols], target.at[leaf, :, mine, cols],
            xs_sem.at[i], xr_sem.at[i], peers[0],
        )
        copy.start()
        sends.append(copy)
        waits.append(
            remote(
                source.at[leaf, other, :, :, cols], target.at[leaf, :, theirs, cols],
                xs_sem.at[i], xr_sem.at[i], peers[0],
            )
        )

    for load in loads:
        load.wait()
    remote(contrast, cbuf.at[box, other], xs_sem.at[8], xr_sem.at[8], peers[0]).wait_recv()
    for d in range(3):
        copy = remote(cbuf.at[box], cbuf.at[box], cs_sem.at[d], cr_sem.at[box], {"box": boxes[d]})
        copy.start()
        sends.append(copy)
    for d in range(3):
        slot = cbuf.at[boxes[d]]
        remote(slot, slot, cs_sem.at[d], cr_sem.at[boxes[d]], {"box": boxes[d]}).wait_recv()
    number = wave[row]
    squared = number * number
    weight = []
    for leaf in range(2):
        stored = order[box * 2 + leaf]
        total = jnp.zeros((2, H), F32)
        for j in range(8):
            total = total + jnp.where(stored == j, cbuf[j // 2, :, j % 2, :], 0.0)
        total = total * squared
        weight.append(
            jnp.concatenate([jnp.broadcast_to(total[i : i + 1], (H, H)).T for i in range(2)], axis=0)
        )

    for copy in waits[:4]:
        copy.wait_recv()

    def lift_op(leaf, cols):
        real, imag = lbuf[leaf, 0, :, cols].T, lbuf[leaf, 1, :, cols].T
        upper = jnp.concatenate([real, -imag], axis=1)
        return halves(jnp.concatenate([upper, jnp.concatenate([imag, real], axis=1)], axis=0))

    def weighted(leaf, cols):
        both = [pbuf[leaf, part, :, cols] * weight[leaf] for part in range(2)]
        return halves(jnp.concatenate(both, axis=0))

    def based(leaf, rows, cols):
        return jnp.concatenate([bbuf[leaf, 0, rows, cols], bbuf[leaf, 1, rows, cols]], axis=0)

    op3 = [lift_op(leaf, high) for leaf in range(2)]
    w3 = [weighted(leaf, high) for leaf in range(2)]
    a33, b33 = [based(leaf, high, high) + mm(op3[leaf], w3[leaf]) for leaf in range(2)]
    op_a33, op_b33 = halves(blk(a33)), halves(blk(b33))
    op = halves(blk(mm(op_b33, halves(a33))))
    for copy in waits[4:6]:
        copy.wait_recv()
    w1 = [weighted(leaf, low) for leaf in range(2)]
    a31, b32 = [based(leaf, high, low) + mm(op3[leaf], w1[leaf]) for leaf in range(2)]
    reach, echo = incoming_maps(op_a33, op, mm(op_b33, halves(a31)), a31, b32)
    for copy in waits[6:]:
        copy.wait_recv()
    op1 = [lift_op(leaf, low) for leaf in range(2)]
    a13, b23 = [based(leaf, low, high) + mm(op1[leaf], w3[leaf]) for leaf in range(2)]
    a11, b22 = [based(leaf, low, low) + mm(op1[leaf], w1[leaf]) for leaf in range(2)]
    bottom = mm(halves(blk(b23)), halves(echo))
    top = mm(halves(blk(a13)), halves(reach))
    top_left, top_right = top[:, :H] + a11, top[:, H:]
    low_left, low_right = bottom[:, :H], bottom[:, H:] + b22
    own[0] = low_right
    own[1] = low_left
    own[2] = top_right
    def illum_half(ref, part):
        rows = pl.ds(part * H, H)
        return jnp.concatenate([ref[0, :, rows].T, ref[1, :, rows].T], axis=0)

    i1, j2 = illum_half(illum, 0), illum_half(illum, 1)
    upper_pair = pair == 1
    east = side == 1
    given = jnp.where(upper_pair, j2, i1)

    swaps = [remote(own.at[i], got.at[i], zs_sem.at[i], zr_sem.at[i], {"box": mate}) for i in range(3)]
    ahead = remote(evec, gvec, es_sem, er_sem, {"box": mate})
    sends += swaps
    swaps[0].start()

    @pl.when(side == 0)
    def _():
        evec[...] = pack(mm(halves(blk(low_left)), halves(given)))
        ahead.start()

    @pl.when(east)
    def _():
        swaps[1].start()

    store_halves(inc1.at[0], wide(reach))
    store_halves(inc1.at[1], wide(echo))
    to_l3, to_k3 = adjoint_maps(a13, a33, b23, b33)
    store_halves(adj1.at[0], to_l3)
    store_halves(adj1.at[1], to_k3)

    @pl.when(side == 0)
    def _():
        swaps[1].start()

    swaps[2].start()

    swaps[0].wait_recv()
    a33, b33 = jnp.where(east, got[0], low_right), jnp.where(east, low_right, got[0])
    op_a33, op_b33 = halves(blk(a33)), halves(blk(b33))
    op = halves(blk(mm(op_b33, halves(a33))))
    far, mid, first = {"box": 4 - box}, {"box": 2}, {"box": 0}
    tops = []
    for i, (where, slot) in enumerate([(far, pair), (mid, pair), (first, 0), (first, 1)]):
        tops.append(
            [
                remote(t33.at[slot], t33.at[slot], ts_sem.at[i], tr_sem.at[slot], where),
                remote(tvec.at[slot], tvec.at[slot], us_sem.at[i], ur_sem.at[slot], where),
            ]
        )

    @pl.when(east)
    def _():
        ahead.wait_recv()
        enter = unpack(gvec[...])
        seen = jnp.concatenate([low_left, mm(op_b33, halves(enter))], axis=1)
        seen = mm(op_a33, halves(apply_iterate(op, seen)))
        seen = jnp.concatenate([seen[:, :H], seen[:, H:] + enter], axis=1)
        seen = mm(halves(blk(top_right)), halves(seen))
        t33[pair] = seen[:, :H] + top_left
        tvec[pair] = pack(seen[:, H:])
        for copy in tops[0] + tops[1]:
            copy.start()

    @pl.when(box == 1)
    def _():
        for copy in tops[2]:
            copy.start()

    swaps[1].wait_recv()
    a31, b32 = jnp.where(east, got[1], low_left), jnp.where(east, low_left, got[1])
    reach, echo = incoming_maps(op_a33, op, mm(op_b33, halves(a31)), a31, b32)

    @pl.when(side == 0)
    def _():
        half_map = mm(halves(blk(top_right)), halves(reach))
        right = blk(half_map[:, H:])
        store_halves(opl, blk(half_map[:, :H] + top_left))
        store_halves(opr, right)
        store_halves(oprt, right.T)

    store_halves(inc2, wide(jnp.where(east, echo, reach)))
    swaps[2].wait_recv()
    a13, b23 = jnp.where(east, got[2], top_right), jnp.where(east, top_right, got[2])
    to_l3, to_k3 = adjoint_maps(a13, a33, b23, b33)
    store_halves(adj2, jnp.where(east, to_k3, to_l3))

    for s in range(2):

        @pl.when(box != 2 * s + 1)
        def _():
            where = {"box": boxes[0]}
            remote(t33.at[s], t33.at[s], ts_sem.at[0], tr_sem.at[s], where).wait_recv()
            remote(tvec.at[s], tvec.at[s], us_sem.at[0], ur_sem.at[s], where).wait_recv()

    @pl.when(box == 1)
    def _():
        for copy in tops[3]:
            copy.start()

    a33, b33 = t33[0], t33[1]
    enter = unpack(tvec[0])
    full_a33, full_b33 = blk(a33), blk(b33)
    op_a33, op_b33 = halves(full_a33), halves(full_b33)
    op = halves(blk(mm(op_b33, halves(a33))))
    i3 = apply_iterate(op, mm(op_b33, halves(enter)) + unpack(tvec[1]))
    j3 = enter + mm(op_a33, halves(i3))
    inner = jnp.where(upper_pair, j3, i3)

    @pl.when(side == 0)
    def _():
        goal = jnp.where(upper_pair, illum_half(observed, 1), illum_half(observed, 0))
        misfit = mm(load_halves(opl), halves(given)) + mm(load_halves(opr), halves(inner)) - goal
        mbuf[...] = pack(misfit)
        vbuf[pair] = pack(mm(load_halves(oprt), halves(misfit)))
        for d in range(3):
            remote(vbuf.at[pair], vbuf.at[pair], vs_sem.at[d], vr_sem.at[pair], {"box": boxes[d]}).start()
        remote(mbuf, mbuf, ms_sem, mr_sem, {"box": mate}).start()

    flip_a33, flip_b33 = full_a33.T, full_b33.T
    op_at, op_bt = halves(flip_a33), halves(flip_b33)
    op = halves(blk(mm(op_bt, halves(flip_a33[:, :H]))))

    for s in range(2):

        @pl.when(box != 2 * s)
        def _():
            remote(vbuf.at[s], vbuf.at[s], vs_sem.at[0], vr_sem.at[s], {"box": boxes[0]}).wait_recv()

    crossed = unpack(vbuf[0])
    l3 = apply_iterate(op, mm(op_bt, halves(crossed)) + unpack(vbuf[1]))
    k3 = crossed + mm(op_at, halves(l3))

    @pl.when(east)
    def _():
        remote(mbuf, mbuf, ms_sem, mr_sem, {"box": mate}).wait_recv()

    back = unpack(mbuf[...])
    below = jnp.where(upper_pair, k3, l3)
    inner_in = mm(load_halves(inc2), halves(jnp.concatenate([given, inner], axis=0)))
    inner_back = mm(load_halves(adj2), halves(jnp.concatenate([back, below], axis=0)))
    in_outer = jnp.where(east, inner, given)
    back_outer = jnp.where(east, below, back)
    split_in = halves(jnp.concatenate([in_outer, inner_in], axis=0))
    split_back = halves(jnp.concatenate([back_outer, inner_back], axis=0))

    ones = jnp.ones((8, 32), jnp.bfloat16)
    across = (((1,), (1,)), ((), ()))
    for leaf in range(2):
        outer_in = inner_in if leaf else in_outer
        outer_back = inner_back if leaf else back_outer
        leaf_in = mm(load_halves(inc1.at[leaf]), split_in)
        leaf_back = mm(load_halves(adj1.at[leaf]), split_back)
        in_re = jnp.concatenate([outer_in[:H], leaf_in[:H]], axis=0)
        in_im = jnp.concatenate([outer_in[H:], leaf_in[H:]], axis=0)
        back_re = jnp.concatenate([outer_back[:H], leaf_back[:H]], axis=0)
        back_im = jnp.concatenate([outer_back[H:], leaf_back[H:]], axis=0)
        probe_in = jnp.concatenate(
            [jnp.concatenate([in_re, in_im], axis=1), jnp.concatenate([-in_im, in_re], axis=1)], axis=0
        )
        lift_in = jnp.concatenate(
            [jnp.concatenate([back_re, -back_im], axis=1), jnp.concatenate([back_im, back_re], axis=1)], axis=0
        )
        lifted = mm(halves(jnp.concatenate([lbuf[leaf, 0], lbuf[leaf, 1]], axis=1)), halves(lift_in))
        probed = mm(halves(jnp.concatenate([pbuf[leaf, 0], pbuf[leaf, 1]], axis=1)), halves(probe_in))
        contrib = lifted[:, :32] * probed[:, :32] - lifted[:, 32:] * probed[:, 32:]
        contrib = halves(contrib * squared)
        summed = [lax.dot_general(ones, part, across, preferred_element_type=F32) for part in contrib]
        summed = summed[0] + summed[1]
        gpart[0, leaf : leaf + 1, :] = summed[0:1, :H]
        gpart[1, leaf : leaf + 1, :] = summed[0:1, H:]

    place = row * 2 + core
    grecv[place] = gpart[row]
    ends = []
    for d, (r, c) in enumerate([(other, core), (row, 1 - core), (other, 1 - core)]):
        copy = remote(gpart.at[r], grecv.at[place], gs_sem.at[d], gr_sem.at[place], peers[d])
        copy.start()
        sends.append(copy)
        slot = grecv.at[r * 2 + c]
        ends.append(remote(slot, slot, gs_sem.at[d], gr_sem.at[r * 2 + c], peers[d]))
    for copy in ends:
        copy.wait_recv()
    gtot[box] = (grecv[0] + grecv[1]) + (grecv[2] + grecv[3])
    for d in range(3):
        copy = remote(gtot.at[box], gtot.at[box], hs_sem.at[d], hr_sem.at[box], {"box": boxes[d]})
        copy.start()
        sends.append(copy)
    for d in range(3):
        slot = gtot.at[boxes[d]]
        remote(slot, slot, hs_sem.at[d], hr_sem.at[boxes[d]], {"box": boxes[d]}).wait_recv()
    for j in range(2):
        total = jnp.zeros((1, H), F32)
        for t in range(8):
            total = total + jnp.where(order[t] == box * 2 + j, gtot[t // 2, t % 2 : t % 2 + 1, :], 0.0)
        out[j : j + 1, :] = total

    for copy in sends:
        copy.wait_send()

    @pl.when(east)
    def _():
        for copy in tops[0] + tops[1]:
            copy.wait_send()

    @pl.when(box == 1)
    def _():
        for copy in tops[2] + tops[3]:
            copy.wait_send()

    @pl.when(side == 0)
    def _():
        for d in range(3):
            remote(vbuf.at[pair], vbuf.at[pair], vs_sem.at[d], vr_sem.at[pair], {"box": boxes[d]}).wait_send()
        remote(mbuf, mbuf, ms_sem, mr_sem, {"box": mate}).wait_send()
        ahead.wait_send()


def fused(*args):
    half = jnp.bfloat16
    dma = pltpu.SemaphoreType.DMA
    scratch = [
        pltpu.SMEM((2,), F32),
        pltpu.SMEM((8,), jnp.int32),
        pltpu.VMEM((2, 32, 2 * H), F32),
        pltpu.VMEM((2, 32, 2 * H), F32),
        pltpu.VMEM((2, 2 * H, 2 * H), half),
        pltpu.VMEM((2, 2 * H, 2 * H), half),
        pltpu.VMEM((2, 2 * H, 2 * H), half),
        pltpu.VMEM((H // 2, H), F32),
        pltpu.VMEM((H // 2, H), F32),
        dma(()),
        dma(()),
        pltpu.VMEM((2, 2, 2 * H, 2 * H), F32),
        pltpu.VMEM((2, 2, 2 * H, 2 * H), F32),
        pltpu.VMEM((2, 2, 2 * H, 2 * H), F32),
        pltpu.VMEM((4, 2, 2, H), F32),
        pltpu.VMEM((3, 2 * H, H), F32),
        pltpu.VMEM((3, 2 * H, H), F32),
        pltpu.VMEM((2, 2 * H, H), F32),
        pltpu.VMEM((2, H // 2, H), F32),
        pltpu.VMEM((H // 2, H), F32),
        pltpu.VMEM((2, H // 2, H), F32),
        pltpu.VMEM((2, 2, 2 * H, 4 * H), half),
        pltpu.VMEM((2, 2, 2 * H, 4 * H), half),
        pltpu.VMEM((2, 2 * H, 4 * H), half),
        pltpu.VMEM((2, 2 * H, 4 * H), half),
        pltpu.VMEM((2, 2, H), F32),
        pltpu.VMEM((4, 2, H), F32),
        pltpu.VMEM((4, 2, H), F32),
        dma((11,)), dma((9,)), dma((9,)), dma((3,)), dma((4,)), dma((3,)), dma((3,)),
        dma((4,)), dma((2,)), dma((4,)), dma((2,)), dma(()), dma(()), dma((3,)), dma((2,)),
        dma((3,)), dma((4,)), dma((3,)), dma((4,)),
    ]
    hbm, vmem = [pl.BlockSpec(memory_space=space) for space in (pltpu.HBM, pltpu.VMEM)]
    return pl.pallas_call(
        kernel,
        out_shape=jax.ShapeDtypeStruct((2, H), F32),
        in_specs=[hbm] * 8,
        out_specs=vmem,
        scratch_shapes=scratch,
        compiler_params=pltpu.CompilerParams(
            collective_id=0, has_side_effects=True, vmem_limit_bytes=63 * 2**20
        ),
        name="gradient",
    )(*args[:6], *[jnp.swapaxes(x, -1, -2) for x in args[6:]])


def pick(mesh):
    def local(*args):
        shape = mesh.shape
        fits = shape["box"] == 4 and shape["row"] == 2 and shape["freq"] == 2
        fits = fits and args[0].shape == (2, 2, 2, 256, 256) and args[6].shape == (1, 2, 2, 256, 32)
        return (fused if fits else body)(*args)

    return local


def solution(mesh):
    return jax.shard_map(
        pick(mesh),
        mesh=mesh,
        in_specs=(
            P(("group", "box"), "freq", None, None, None),
            P(("group", "box"), "freq", None, "row", None),
            P(("group", "box"), "freq", None, "row", None),
            P(("group", "freq")),
            P(("group", "box"), "row"),
            P("group"),
            P("group", "freq", None, None, None),
            P("group", "freq", None, None, None),
        ),
        out_specs=P(("group", "box"), "row"),
        check_vma=False,
    )
```

```python
from functools import partial

import jax
import jax.numpy as jnp
from jax import lax
from jax.experimental import pallas as pl
from jax.experimental.pallas import tpu as pltpu
from jax.sharding import PartitionSpec as P

LEVELS = 3


def from_partner(block, axis, apart):
    count = lax.axis_size(axis)
    route = []
    for low in range(count):
        high = low | 1 << apart
        if high != low and high < count:
            route += [(low, high), (high, low)]
    return lax.ppermute(block, axis, route)


def complex_mul(matrix_a, matrix_b):
    product = partial(jnp.matmul, precision=lax.Precision.HIGHEST)
    real_a, imag_a = (matrix_a[..., 0, :, :], matrix_a[..., 1, :, :])
    real_b, imag_b = (matrix_b[..., 0, :, :], matrix_b[..., 1, :, :])
    return jnp.stack(
        [
            product(real_a, real_b) - product(imag_a, imag_b),
            product(real_a, imag_b) + product(imag_a, real_b),
        ],
        axis=-3,
    )


def conj_transpose(matrix):
    return jnp.stack(
        [jnp.swapaxes(matrix[..., 0, :, :], -1, -2), -jnp.swapaxes(matrix[..., 1, :, :], -1, -2)],
        axis=-3,
    )


def approx_inverse(coupled):
    real_part = coupled[..., 0, :, :]
    unit = jnp.broadcast_to(jnp.eye(coupled.shape[-1], dtype=coupled.dtype), real_part.shape)
    identity = jnp.stack([unit, jnp.zeros_like(real_part)], axis=-3)
    system = identity - coupled
    iterate = identity + coupled
    iterate = complex_mul(iterate, 2.0 * identity - complex_mul(system, iterate))
    return iterate


def split_blocks(matrix, half):
    return (
        matrix[..., :half, :half],
        matrix[..., :half, half:],
        matrix[..., half:, :half],
        matrix[..., half:, half:],
    )


def merge_pair(west, east):
    half = west.shape[-1] // 2
    west_outer, west_cross, west_enter, west_inner = split_blocks(west, half)
    east_outer, east_cross, east_enter, east_inner = split_blocks(east, half)
    forward_inv = approx_inverse(complex_mul(east_inner, west_inner))
    backward_inv = approx_inverse(complex_mul(west_inner, east_inner))
    reach_west = complex_mul(forward_inv, complex_mul(east_inner, west_enter))
    reach_east = complex_mul(forward_inv, east_enter)
    echo_west = west_enter + complex_mul(west_inner, reach_west)
    echo_east = complex_mul(west_inner, reach_east)
    top_rows = jnp.concatenate(
        [west_outer + complex_mul(west_cross, reach_west), complex_mul(west_cross, reach_east)],
        axis=-1,
    )
    bottom_rows = jnp.concatenate(
        [complex_mul(east_cross, echo_west), east_outer + complex_mul(east_cross, echo_east)],
        axis=-1,
    )
    return (jnp.concatenate([top_rows, bottom_rows], axis=-2), forward_inv, backward_inv)


def descend_pair(west, east, forward_inv, backward_inv, incoming, adjoint):
    half = west.shape[-1] // 2
    west_outer, west_cross, west_enter, west_inner = split_blocks(west, half)
    east_outer, east_cross, east_enter, east_inner = split_blocks(east, half)
    given_west, given_east = (incoming[..., :half, :], incoming[..., half:, :])
    back_west, back_east = (adjoint[..., :half, :], adjoint[..., half:, :])
    into_west = complex_mul(west_enter, given_west)
    west_in = complex_mul(
        forward_inv, complex_mul(east_inner, into_west) + complex_mul(east_enter, given_east)
    )
    east_in = into_west + complex_mul(west_inner, west_in)
    crossed = complex_mul(conj_transpose(west_cross), back_west)
    west_back = complex_mul(
        conj_transpose(backward_inv),
        complex_mul(conj_transpose(east_inner), crossed)
        + complex_mul(conj_transpose(east_cross), back_east),
    )
    east_back = crossed + complex_mul(conj_transpose(west_inner), west_back)
    west_side = (
        jnp.concatenate([given_west, west_in], axis=-2),
        jnp.concatenate([back_west, west_back], axis=-2),
    )
    east_side = (
        jnp.concatenate([given_east, east_in], axis=-2),
        jnp.concatenate([back_east, east_back], axis=-2),
    )
    return (west_side, east_side)


def alternate(west, east):
    stacked = jnp.stack([west, east], axis=1)
    return stacked.reshape((-1,) + west.shape[1:])


def body(
    base_maps, lift_rows, probe_rows, wavenumber, contrast, tree_order, illumination, observed
):
    highest = lax.Precision.HIGHEST
    leaf_count = contrast.shape[0]
    tree_depth = leaf_count.bit_length() - 1
    box_index = lax.axis_index("box")
    positions = box_index * leaf_count + jnp.arange(leaf_count, dtype=jnp.int32)
    mine_order = jnp.take(tree_order, positions)
    every_contrast = lax.all_gather(contrast, "box", axis=0, tiled=True)
    selector = (
        mine_order[:, None] == jnp.arange(every_contrast.shape[0], dtype=jnp.int32)[None, :]
    ).astype(jnp.float32)
    tree_contrast = jnp.matmul(selector, every_contrast, precision=highest)
    squared = wavenumber * wavenumber
    weighted = (
        tree_contrast[:, None, None, :, None] * probe_rows * squared[None, :, None, None, None]
    )
    lift_swapped = jnp.swapaxes(lift_rows, -1, -2)
    node_maps = base_maps + lax.psum(complex_mul(lift_swapped, weighted), "row")
    saved = []
    whole_map = node_maps
    for level in range(LEVELS):
        if node_maps.shape[0] >= 2:
            former = node_maps[0::2]
            latter = node_maps[1::2]
            side_flag = None
        else:
            bit_index = level - tree_depth
            sibling = from_partner(node_maps, "box", bit_index)
            side_flag = box_index // 2**bit_index % 2
            former = jnp.where(side_flag == 0, node_maps, sibling)
            latter = jnp.where(side_flag == 0, sibling, node_maps)
        whole_map, forward_inv, backward_inv = merge_pair(former, latter)
        saved.append((former, latter, forward_inv, backward_inv, side_flag))
        node_maps = whole_map
    top_index = box_index * leaf_count // 8
    incoming = lax.dynamic_slice_in_dim(illumination, top_index, 1, 0)
    target = lax.dynamic_slice_in_dim(observed, top_index, 1, 0)
    adjoint = complex_mul(whole_map, incoming) - target
    for former, latter, forward_inv, backward_inv, side_flag in reversed(saved):
        west_side, east_side = descend_pair(
            former, latter, forward_inv, backward_inv, incoming, adjoint
        )
        if side_flag is None:
            incoming = alternate(west_side[0], east_side[0])
            adjoint = alternate(west_side[1], east_side[1])
        else:
            incoming = jnp.where(side_flag == 0, west_side[0], east_side[0])
            adjoint = jnp.where(side_flag == 0, west_side[1], east_side[1])
    conj_adjoint = jnp.stack([adjoint[..., 0, :, :], -adjoint[..., 1, :, :]], axis=-3)
    lifted = complex_mul(lift_rows, conj_adjoint)
    probed = complex_mul(probe_rows, incoming)
    contrib = lifted[:, :, 0] * probed[:, :, 0] - lifted[:, :, 1] * probed[:, :, 1]
    partial_grad = jnp.einsum("lfks,f->lk", contrib, squared, precision=highest)
    total = lax.psum(partial_grad, "freq")
    rows_here = jnp.arange(lax.axis_size("box") * leaf_count, dtype=jnp.int32)
    chooser = (rows_here[:, None] == mine_order[None, :]).astype(jnp.float32)
    return lax.psum_scatter(
        jnp.matmul(chooser, total, precision=highest), "box", scatter_dimension=0, tiled=True
    )


H = 128
MESH = pl.DeviceIdType.MESH
F32 = jnp.float32


def halves(x):
    high = x.astype(jnp.bfloat16)
    return high, (x - high.astype(F32)).astype(jnp.bfloat16)


def mm(a, b):
    dot = partial(jnp.dot, preferred_element_type=F32)
    return dot(a[0], b[0]) + (dot(a[0], b[1]) + dot(a[1], b[0]))


def blk(x):
    turned = jnp.concatenate([-x[H:], x[:H]], axis=0)
    return jnp.concatenate([x, turned], axis=1)


def apply_iterate(op, x):
    once = mm(op, halves(x))
    even = x + mm(op, halves(once))
    return even + mm(op, halves(even))


def pack(x):
    q = x.shape[0] // 4
    return jnp.concatenate([x[i * q : (i + 1) * q] for i in range(4)], axis=1)


def unpack(x):
    q = x.shape[1] // 4
    return jnp.concatenate([x[:, i * q : (i + 1) * q] for i in range(4)], axis=0)


def adjoint_maps(a13, a33, b23, b33):
    op_a33, op_a13, op_b23 = halves(blk(a33)), halves(blk(a13)), halves(blk(b23))
    split_b33, split_a33 = halves(b33), halves(a33)
    coupled = mm(op_a33, split_b33)
    op = halves(blk(coupled))
    row = lax.broadcasted_iota(jnp.int32, (2 * H, H), 0)
    col = lax.broadcasted_iota(jnp.int32, (2 * H, H), 1)
    even = jnp.where(row == col, 1.0, 0.0) + mm(op, halves(coupled))
    inverse = halves(even + mm(op, halves(even)))
    f1 = blk(mm(halves(blk(mm(op_a13, split_b33))), inverse))
    f2 = blk(mm(op_b23, inverse))
    g1 = blk(a13 + mm(halves(f1), split_a33))
    g2 = blk(mm(halves(f2), split_a33))
    to_l3 = jnp.concatenate([f1.T, f2.T], axis=1)
    to_k3 = jnp.concatenate([g1.T, g2.T], axis=1)
    return to_l3, to_k3


def incoming_maps(op_a33, op, b33a31, a31, b32):
    reach = apply_iterate(op, jnp.concatenate([b33a31, b32], axis=1))
    echo = mm(op_a33, halves(reach))
    return reach, jnp.concatenate([echo[:, :H] + a31, echo[:, H:]], axis=1)


def wide(x):
    return jnp.concatenate([blk(x[:, :H]), blk(x[:, H:])], axis=1)


def store_halves(ref, x):
    high, low = halves(x)
    ref[0] = high
    ref[1] = low


def load_halves(ref):
    return ref[0], ref[1]


def kernel(
    base, lift, probe, wave_in, contrast, order_in, illum_in, observed_in, out,
    wave, order, illum, observed, opl, opr, oprt, evec, gvec, es_sem, er_sem,
    lbuf, pbuf, bbuf, cbuf, own, got, t33, tvec, mbuf, vbuf, inc1, adj1, inc2, adj2,
    gpart, grecv, loc_sem, xs_sem, xr_sem, cs_sem, cr_sem, zs_sem, zr_sem,
    ts_sem, tr_sem, us_sem, ur_sem, ms_sem, mr_sem, vs_sem, vr_sem, gs_sem, gr_sem,
):
    box = lax.axis_index("box")
    row = lax.axis_index("row")
    core = lax.axis_index("freq")
    side = lax.rem(box, 2)
    pair = box // 2
    mate = box + 1 - 2 * side
    other = 1 - row
    boxes = [lax.rem(box + d, 4) for d in (1, 2, 3)]
    peers = [{"row": other, "freq": core}, {"row": row, "freq": 1 - core}, {"row": other, "freq": 1 - core}]

    def remote(source, target, sender, receiver, where):
        return pltpu.make_async_remote_copy(
            src_ref=source, dst_ref=target, send_sem=sender, recv_sem=receiver,
            device_id=where, device_id_type=MESH,
        )

    mine = pl.ds(pl.multiple_of(row * H, H), H)
    theirs = pl.ds(pl.multiple_of(other * H, H), H)
    loads = []
    for leaf in range(2):
        loads += [
            (lift.at[leaf, row], lbuf.at[leaf, :, mine, :]),
            (probe.at[leaf, row], pbuf.at[leaf, :, mine, :]),
            (base.at[leaf, row], bbuf.at[leaf]),
        ]
    loads += [(wave_in, wave), (order_in, order), (illum_in.at[0, row], illum)]
    loads += [(observed_in.at[0, row], observed), (contrast, cbuf.at[box, row])]
    loads = [pltpu.make_async_copy(s, t, loc_sem.at[i]) for i, (s, t) in enumerate(loads)]
    for load in loads:
        load.start()

    barrier = pltpu.get_barrier_semaphore()
    others = []
    for d in (2, 1, 3, 0):
        for i in range(2):
            for j in range(2):
                if d + i + j > 0:
                    place = lax.rem(box + d, 4), lax.rem(row + i, 2), lax.rem(core + j, 2)
                    others.append(dict(zip(("box", "row", "freq"), place)))
    for where in others:
        pl.semaphore_signal(barrier, inc=1, device_id=where, device_id_type=MESH)
    pl.semaphore_wait(barrier, 15)

    early = remote(contrast, cbuf.at[box, row], xs_sem.at[8], xr_sem.at[8], peers[0])
    early.start()
    low, high = pl.ds(0, H), pl.ds(H, H)
    plan = [(lift, lbuf, 0, high), (probe, pbuf, 0, high), (lift, lbuf, 1, high), (probe, pbuf, 1, high)]
    plan += [(probe, pbuf, 0, low), (probe, pbuf, 1, low), (lift, lbuf, 0, low), (lift, lbuf, 1, low)]
    sends, waits = [early], []
    for i, (source, target, leaf, cols) in enumerate(plan):
        copy = remote(
            source.at[leaf, other, :, :, cols], target.at[leaf, :, mine, cols],
            xs_sem.at[i], xr_sem.at[i], peers[0],
        )
        copy.start()
        sends.append(copy)
        waits.append(
            remote(
                source.at[leaf, other, :, :, cols], target.at[leaf, :, theirs, cols],
                xs_sem.at[i], xr_sem.at[i], peers[0],
            )
        )

    for load in loads:
        load.wait()
    remote(contrast, cbuf.at[box, other], xs_sem.at[8], xr_sem.at[8], peers[0]).wait_recv()
    for d in range(3):
        copy = remote(cbuf.at[box], cbuf.at[box], cs_sem.at[d], cr_sem.at[box], {"box": boxes[d]})
        copy.start()
        sends.append(copy)
    for d in range(3):
        slot = cbuf.at[boxes[d]]
        remote(slot, slot, cs_sem.at[d], cr_sem.at[boxes[d]], {"box": boxes[d]}).wait_recv()
    number = wave[row]
    squared = number * number
    weight = []
    for leaf in range(2):
        stored = order[box * 2 + leaf]
        total = jnp.zeros((2, H), F32)
        for j in range(8):
            total = total + jnp.where(stored == j, cbuf[j // 2, :, j % 2, :], 0.0)
        total = total * squared
        weight.append(
            jnp.concatenate([jnp.broadcast_to(total[i : i + 1], (H, H)).T for i in range(2)], axis=0)
        )

    for copy in waits[:4]:
        copy.wait_recv()

    def lift_op(leaf, cols):
        real, imag = lbuf[leaf, 0, :, cols].T, lbuf[leaf, 1, :, cols].T
        upper = jnp.concatenate([real, -imag], axis=1)
        return halves(jnp.concatenate([upper, jnp.concatenate([imag, real], axis=1)], axis=0))

    def weighted(leaf, cols):
        both = [pbuf[leaf, part, :, cols] * weight[leaf] for part in range(2)]
        return halves(jnp.concatenate(both, axis=0))

    def based(leaf, rows, cols):
        return jnp.concatenate([bbuf[leaf, 0, rows, cols], bbuf[leaf, 1, rows, cols]], axis=0)

    op3 = [lift_op(leaf, high) for leaf in range(2)]
    w3 = [weighted(leaf, high) for leaf in range(2)]
    a33, b33 = [based(leaf, high, high) + mm(op3[leaf], w3[leaf]) for leaf in range(2)]
    op_a33, op_b33 = halves(blk(a33)), halves(blk(b33))
    op = halves(blk(mm(op_b33, halves(a33))))
    for copy in waits[4:6]:
        copy.wait_recv()
    w1 = [weighted(leaf, low) for leaf in range(2)]
    a31, b32 = [based(leaf, high, low) + mm(op3[leaf], w1[leaf]) for leaf in range(2)]
    reach, echo = incoming_maps(op_a33, op, mm(op_b33, halves(a31)), a31, b32)
    for copy in waits[6:]:
        copy.wait_recv()
    op1 = [lift_op(leaf, low) for leaf in range(2)]
    a13, b23 = [based(leaf, low, high) + mm(op1[leaf], w3[leaf]) for leaf in range(2)]
    a11, b22 = [based(leaf, low, low) + mm(op1[leaf], w1[leaf]) for leaf in range(2)]
    bottom = mm(halves(blk(b23)), halves(echo))
    top = mm(halves(blk(a13)), halves(reach))
    top_left, top_right = top[:, :H] + a11, top[:, H:]
    low_left, low_right = bottom[:, :H], bottom[:, H:] + b22
    own[0] = low_right
    own[1] = low_left
    own[2] = top_right
    def illum_half(ref, part):
        rows = pl.ds(part * H, H)
        return jnp.concatenate([ref[0, :, rows].T, ref[1, :, rows].T], axis=0)

    i1, j2 = illum_half(illum, 0), illum_half(illum, 1)
    upper_pair = pair == 1
    east = side == 1
    given = jnp.where(upper_pair, j2, i1)

    swaps = [remote(own.at[i], got.at[i], zs_sem.at[i], zr_sem.at[i], {"box": mate}) for i in range(3)]
    ahead = remote(evec, gvec, es_sem, er_sem, {"box": mate})
    sends += swaps
    swaps[0].start()

    @pl.when(side == 0)
    def _():
        evec[...] = pack(mm(halves(blk(low_left)), halves(given)))
        ahead.start()

    @pl.when(east)
    def _():
        swaps[1].start()

    store_halves(inc1.at[0], wide(reach))
    store_halves(inc1.at[1], wide(echo))
    to_l3, to_k3 = adjoint_maps(a13, a33, b23, b33)
    store_halves(adj1.at[0], to_l3)
    store_halves(adj1.at[1], to_k3)

    @pl.when(side == 0)
    def _():
        swaps[1].start()

    swaps[2].start()

    swaps[0].wait_recv()
    a33, b33 = jnp.where(east, got[0], low_right), jnp.where(east, low_right, got[0])
    op_a33, op_b33 = halves(blk(a33)), halves(blk(b33))
    op = halves(blk(mm(op_b33, halves(a33))))
    far, mid, first = {"box": 4 - box}, {"box": 2}, {"box": 0}
    tops = []
    for i, (where, slot) in enumerate([(far, pair), (mid, pair), (first, 0), (first, 1)]):
        tops.append(
            [
                remote(t33.at[slot], t33.at[slot], ts_sem.at[i], tr_sem.at[slot], where),
                remote(tvec.at[slot], tvec.at[slot], us_sem.at[i], ur_sem.at[slot], where),
            ]
        )

    @pl.when(east)
    def _():
        ahead.wait_recv()
        enter = unpack(gvec[...])
        seen = jnp.concatenate([low_left, mm(op_b33, halves(enter))], axis=1)
        seen = mm(op_a33, halves(apply_iterate(op, seen)))
        seen = jnp.concatenate([seen[:, :H], seen[:, H:] + enter], axis=1)
        seen = mm(halves(blk(top_right)), halves(seen))
        t33[pair] = seen[:, :H] + top_left
        tvec[pair] = pack(seen[:, H:])
        for copy in tops[0]:
            copy.start()

    @pl.when(box == 1)
    def _():
        for copy in tops[2]:
            copy.start()

    swaps[1].wait_recv()
    a31, b32 = jnp.where(east, got[1], low_left), jnp.where(east, low_left, got[1])
    reach, echo = incoming_maps(op_a33, op, mm(op_b33, halves(a31)), a31, b32)

    @pl.when(east)
    def _():
        for copy in tops[1]:
            copy.start()

    @pl.when(side == 0)
    def _():
        half_map = mm(halves(blk(top_right)), halves(reach))
        right = blk(half_map[:, H:])
        store_halves(opl, blk(half_map[:, :H] + top_left))
        store_halves(opr, right)
        store_halves(oprt, right.T)

    store_halves(inc2, wide(jnp.where(east, echo, reach)))
    swaps[2].wait_recv()
    a13, b23 = jnp.where(east, got[2], top_right), jnp.where(east, top_right, got[2])
    to_l3, to_k3 = adjoint_maps(a13, a33, b23, b33)
    store_halves(adj2, jnp.where(east, to_k3, to_l3))

    for s in range(2):

        @pl.when(box != 2 * s + 1)
        def _():
            where = {"box": boxes[0]}
            remote(t33.at[s], t33.at[s], ts_sem.at[0], tr_sem.at[s], where).wait_recv()
            remote(tvec.at[s], tvec.at[s], us_sem.at[0], ur_sem.at[s], where).wait_recv()

    @pl.when(box == 1)
    def _():
        for copy in tops[3]:
            copy.start()

    a33, b33 = t33[0], t33[1]
    enter = unpack(tvec[0])
    full_a33, full_b33 = blk(a33), blk(b33)
    op_a33, op_b33 = halves(full_a33), halves(full_b33)
    op = halves(blk(mm(op_b33, halves(a33))))
    i3 = apply_iterate(op, mm(op_b33, halves(enter)) + unpack(tvec[1]))
    j3 = enter + mm(op_a33, halves(i3))
    inner = jnp.where(upper_pair, j3, i3)

    @pl.when(side == 0)
    def _():
        goal = jnp.where(upper_pair, illum_half(observed, 1), illum_half(observed, 0))
        misfit = mm(load_halves(opl), halves(given)) + mm(load_halves(opr), halves(inner)) - goal
        mbuf[...] = pack(misfit)
        vbuf[pair] = pack(mm(load_halves(oprt), halves(misfit)))
        for d in range(3):
            remote(vbuf.at[pair], vbuf.at[pair], vs_sem.at[d], vr_sem.at[pair], {"box": boxes[d]}).start()
        remote(mbuf, mbuf, ms_sem, mr_sem, {"box": mate}).start()

    flip_a33, flip_b33 = full_a33.T, full_b33.T
    op_at, op_bt = halves(flip_a33), halves(flip_b33)
    op = halves(blk(mm(op_bt, halves(flip_a33[:, :H]))))

    for s in range(2):

        @pl.when(box != 2 * s)
        def _():
            remote(vbuf.at[s], vbuf.at[s], vs_sem.at[0], vr_sem.at[s], {"box": boxes[0]}).wait_recv()

    crossed = unpack(vbuf[0])
    l3 = apply_iterate(op, mm(op_bt, halves(crossed)) + unpack(vbuf[1]))
    k3 = crossed + mm(op_at, halves(l3))

    @pl.when(east)
    def _():
        remote(mbuf, mbuf, ms_sem, mr_sem, {"box": mate}).wait_recv()

    back = unpack(mbuf[...])
    below = jnp.where(upper_pair, k3, l3)
    inner_in = mm(load_halves(inc2), halves(jnp.concatenate([given, inner], axis=0)))
    inner_back = mm(load_halves(adj2), halves(jnp.concatenate([back, below], axis=0)))
    in_outer = jnp.where(east, inner, given)
    back_outer = jnp.where(east, below, back)
    split_in = halves(jnp.concatenate([in_outer, inner_in], axis=0))
    split_back = halves(jnp.concatenate([back_outer, inner_back], axis=0))

    ones = jnp.ones((8, 32), jnp.bfloat16)
    across = (((1,), (1,)), ((), ()))
    for leaf in range(2):
        outer_in = inner_in if leaf else in_outer
        outer_back = inner_back if leaf else back_outer
        leaf_in = mm(load_halves(inc1.at[leaf]), split_in)
        leaf_back = mm(load_halves(adj1.at[leaf]), split_back)
        in_re = jnp.concatenate([outer_in[:H], leaf_in[:H]], axis=0)
        in_im = jnp.concatenate([outer_in[H:], leaf_in[H:]], axis=0)
        back_re = jnp.concatenate([outer_back[:H], leaf_back[:H]], axis=0)
        back_im = jnp.concatenate([outer_back[H:], leaf_back[H:]], axis=0)
        probe_in = jnp.concatenate(
            [jnp.concatenate([in_re, in_im], axis=1), jnp.concatenate([-in_im, in_re], axis=1)], axis=0
        )
        lift_in = jnp.concatenate(
            [jnp.concatenate([back_re, -back_im], axis=1), jnp.concatenate([back_im, back_re], axis=1)], axis=0
        )
        lifted = mm(halves(jnp.concatenate([lbuf[leaf, 0], lbuf[leaf, 1]], axis=1)), halves(lift_in))
        probed = mm(halves(jnp.concatenate([pbuf[leaf, 0], pbuf[leaf, 1]], axis=1)), halves(probe_in))
        contrib = lifted[:, :32] * probed[:, :32] - lifted[:, 32:] * probed[:, 32:]
        contrib = halves(contrib * squared)
        summed = [lax.dot_general(ones, part, across, preferred_element_type=F32) for part in contrib]
        summed = summed[0] + summed[1]
        gpart[0, leaf : leaf + 1, :] = summed[0:1, :H]
        gpart[1, leaf : leaf + 1, :] = summed[0:1, H:]

    place = box * 4 + row * 2 + core
    grecv[place] = gpart[row]
    ends = []
    for i, where in enumerate(others):
        copy = remote(gpart.at[where["row"]], grecv.at[place], gs_sem.at[i], gr_sem.at[place], where)
        copy.start()
        sends.append(copy)
        source = where["box"] * 4 + where["row"] * 2 + where["freq"]
        ends.append(remote(grecv.at[source], grecv.at[source], gs_sem.at[i], gr_sem.at[source], where))
    for copy in ends:
        copy.wait_recv()
    sums = []
    for b in range(4):
        sums.append((grecv[4 * b] + grecv[4 * b + 1]) + (grecv[4 * b + 2] + grecv[4 * b + 3]))
    for j in range(2):
        total = jnp.zeros((1, H), F32)
        for t in range(8):
            total = total + jnp.where(order[t] == box * 2 + j, sums[t // 2][t % 2 : t % 2 + 1, :], 0.0)
        out[j : j + 1, :] = total

    for copy in sends:
        copy.wait_send()

    @pl.when(east)
    def _():
        for copy in tops[0] + tops[1]:
            copy.wait_send()

    @pl.when(box == 1)
    def _():
        for copy in tops[2] + tops[3]:
            copy.wait_send()

    @pl.when(side == 0)
    def _():
        for d in range(3):
            remote(vbuf.at[pair], vbuf.at[pair], vs_sem.at[d], vr_sem.at[pair], {"box": boxes[d]}).wait_send()
        remote(mbuf, mbuf, ms_sem, mr_sem, {"box": mate}).wait_send()
        ahead.wait_send()


def fused(*args):
    half = jnp.bfloat16
    dma = pltpu.SemaphoreType.DMA
    scratch = [
        pltpu.SMEM((2,), F32),
        pltpu.SMEM((8,), jnp.int32),
        pltpu.VMEM((2, 32, 2 * H), F32),
        pltpu.VMEM((2, 32, 2 * H), F32),
        pltpu.VMEM((2, 2 * H, 2 * H), half),
        pltpu.VMEM((2, 2 * H, 2 * H), half),
        pltpu.VMEM((2, 2 * H, 2 * H), half),
        pltpu.VMEM((H // 2, H), F32),
        pltpu.VMEM((H // 2, H), F32),
        dma(()),
        dma(()),
        pltpu.VMEM((2, 2, 2 * H, 2 * H), F32),
        pltpu.VMEM((2, 2, 2 * H, 2 * H), F32),
        pltpu.VMEM((2, 2, 2 * H, 2 * H), F32),
        pltpu.VMEM((4, 2, 2, H), F32),
        pltpu.VMEM((3, 2 * H, H), F32),
        pltpu.VMEM((3, 2 * H, H), F32),
        pltpu.VMEM((2, 2 * H, H), F32),
        pltpu.VMEM((2, H // 2, H), F32),
        pltpu.VMEM((H // 2, H), F32),
        pltpu.VMEM((2, H // 2, H), F32),
        pltpu.VMEM((2, 2, 2 * H, 4 * H), half),
        pltpu.VMEM((2, 2, 2 * H, 4 * H), half),
        pltpu.VMEM((2, 2 * H, 4 * H), half),
        pltpu.VMEM((2, 2 * H, 4 * H), half),
        pltpu.VMEM((2, 2, H), F32),
        pltpu.VMEM((16, 2, H), F32),
        dma((11,)), dma((9,)), dma((9,)), dma((3,)), dma((4,)), dma((3,)), dma((3,)),
        dma((4,)), dma((2,)), dma((4,)), dma((2,)), dma(()), dma(()), dma((3,)), dma((2,)),
        dma((15,)), dma((16,)),
    ]
    hbm, vmem = [pl.BlockSpec(memory_space=space) for space in (pltpu.HBM, pltpu.VMEM)]
    return pl.pallas_call(
        kernel,
        out_shape=jax.ShapeDtypeStruct((2, H), F32),
        in_specs=[hbm] * 8,
        out_specs=vmem,
        scratch_shapes=scratch,
        compiler_params=pltpu.CompilerParams(
            collective_id=0, has_side_effects=True, vmem_limit_bytes=63 * 2**20
        ),
        name="gradient",
    )(*args[:6], *[jnp.swapaxes(x, -1, -2) for x in args[6:]])


def pick(mesh):
    def local(*args):
        shape = mesh.shape
        fits = shape["box"] == 4 and shape["row"] == 2 and shape["freq"] == 2
        fits = fits and args[0].shape == (2, 2, 2, 256, 256) and args[6].shape == (1, 2, 2, 256, 32)
        return (fused if fits else body)(*args)

    return local


def solution(mesh):
    return jax.shard_map(
        pick(mesh),
        mesh=mesh,
        in_specs=(
            P(("group", "box"), "freq", None, None, None),
            P(("group", "box"), "freq", None, "row", None),
            P(("group", "box"), "freq", None, "row", None),
            P(("group", "freq")),
            P(("group", "box"), "row"),
            P("group"),
            P("group", "freq", None, None, None),
            P("group", "freq", None, None, None),
        ),
        out_specs=P(("group", "box"), "row"),
        check_vma=False,
    )
```

```python
from functools import partial

import jax
import jax.numpy as jnp
from jax import lax
from jax.experimental import pallas as pl
from jax.experimental.pallas import tpu as pltpu
from jax.sharding import PartitionSpec as P

LEVELS = 3


def from_partner(block, axis, apart):
    count = lax.axis_size(axis)
    route = []
    for low in range(count):
        high = low | 1 << apart
        if high != low and high < count:
            route += [(low, high), (high, low)]
    return lax.ppermute(block, axis, route)


def complex_mul(matrix_a, matrix_b):
    product = partial(jnp.matmul, precision=lax.Precision.HIGHEST)
    real_a, imag_a = (matrix_a[..., 0, :, :], matrix_a[..., 1, :, :])
    real_b, imag_b = (matrix_b[..., 0, :, :], matrix_b[..., 1, :, :])
    return jnp.stack(
        [
            product(real_a, real_b) - product(imag_a, imag_b),
            product(real_a, imag_b) + product(imag_a, real_b),
        ],
        axis=-3,
    )


def conj_transpose(matrix):
    return jnp.stack(
        [jnp.swapaxes(matrix[..., 0, :, :], -1, -2), -jnp.swapaxes(matrix[..., 1, :, :], -1, -2)],
        axis=-3,
    )


def approx_inverse(coupled):
    real_part = coupled[..., 0, :, :]
    unit = jnp.broadcast_to(jnp.eye(coupled.shape[-1], dtype=coupled.dtype), real_part.shape)
    identity = jnp.stack([unit, jnp.zeros_like(real_part)], axis=-3)
    system = identity - coupled
    iterate = identity + coupled
    iterate = complex_mul(iterate, 2.0 * identity - complex_mul(system, iterate))
    return iterate


def split_blocks(matrix, half):
    return (
        matrix[..., :half, :half],
        matrix[..., :half, half:],
        matrix[..., half:, :half],
        matrix[..., half:, half:],
    )


def merge_pair(west, east):
    half = west.shape[-1] // 2
    west_outer, west_cross, west_enter, west_inner = split_blocks(west, half)
    east_outer, east_cross, east_enter, east_inner = split_blocks(east, half)
    forward_inv = approx_inverse(complex_mul(east_inner, west_inner))
    backward_inv = approx_inverse(complex_mul(west_inner, east_inner))
    reach_west = complex_mul(forward_inv, complex_mul(east_inner, west_enter))
    reach_east = complex_mul(forward_inv, east_enter)
    echo_west = west_enter + complex_mul(west_inner, reach_west)
    echo_east = complex_mul(west_inner, reach_east)
    top_rows = jnp.concatenate(
        [west_outer + complex_mul(west_cross, reach_west), complex_mul(west_cross, reach_east)],
        axis=-1,
    )
    bottom_rows = jnp.concatenate(
        [complex_mul(east_cross, echo_west), east_outer + complex_mul(east_cross, echo_east)],
        axis=-1,
    )
    return (jnp.concatenate([top_rows, bottom_rows], axis=-2), forward_inv, backward_inv)


def descend_pair(west, east, forward_inv, backward_inv, incoming, adjoint):
    half = west.shape[-1] // 2
    west_outer, west_cross, west_enter, west_inner = split_blocks(west, half)
    east_outer, east_cross, east_enter, east_inner = split_blocks(east, half)
    given_west, given_east = (incoming[..., :half, :], incoming[..., half:, :])
    back_west, back_east = (adjoint[..., :half, :], adjoint[..., half:, :])
    into_west = complex_mul(west_enter, given_west)
    west_in = complex_mul(
        forward_inv, complex_mul(east_inner, into_west) + complex_mul(east_enter, given_east)
    )
    east_in = into_west + complex_mul(west_inner, west_in)
    crossed = complex_mul(conj_transpose(west_cross), back_west)
    west_back = complex_mul(
        conj_transpose(backward_inv),
        complex_mul(conj_transpose(east_inner), crossed)
        + complex_mul(conj_transpose(east_cross), back_east),
    )
    east_back = crossed + complex_mul(conj_transpose(west_inner), west_back)
    west_side = (
        jnp.concatenate([given_west, west_in], axis=-2),
        jnp.concatenate([back_west, west_back], axis=-2),
    )
    east_side = (
        jnp.concatenate([given_east, east_in], axis=-2),
        jnp.concatenate([back_east, east_back], axis=-2),
    )
    return (west_side, east_side)


def alternate(west, east):
    stacked = jnp.stack([west, east], axis=1)
    return stacked.reshape((-1,) + west.shape[1:])


def body(
    base_maps, lift_rows, probe_rows, wavenumber, contrast, tree_order, illumination, observed
):
    highest = lax.Precision.HIGHEST
    leaf_count = contrast.shape[0]
    tree_depth = leaf_count.bit_length() - 1
    box_index = lax.axis_index("box")
    positions = box_index * leaf_count + jnp.arange(leaf_count, dtype=jnp.int32)
    mine_order = jnp.take(tree_order, positions)
    every_contrast = lax.all_gather(contrast, "box", axis=0, tiled=True)
    selector = (
        mine_order[:, None] == jnp.arange(every_contrast.shape[0], dtype=jnp.int32)[None, :]
    ).astype(jnp.float32)
    tree_contrast = jnp.matmul(selector, every_contrast, precision=highest)
    squared = wavenumber * wavenumber
    weighted = (
        tree_contrast[:, None, None, :, None] * probe_rows * squared[None, :, None, None, None]
    )
    lift_swapped = jnp.swapaxes(lift_rows, -1, -2)
    node_maps = base_maps + lax.psum(complex_mul(lift_swapped, weighted), "row")
    saved = []
    whole_map = node_maps
    for level in range(LEVELS):
        if node_maps.shape[0] >= 2:
            former = node_maps[0::2]
            latter = node_maps[1::2]
            side_flag = None
        else:
            bit_index = level - tree_depth
            sibling = from_partner(node_maps, "box", bit_index)
            side_flag = box_index // 2**bit_index % 2
            former = jnp.where(side_flag == 0, node_maps, sibling)
            latter = jnp.where(side_flag == 0, sibling, node_maps)
        whole_map, forward_inv, backward_inv = merge_pair(former, latter)
        saved.append((former, latter, forward_inv, backward_inv, side_flag))
        node_maps = whole_map
    top_index = box_index * leaf_count // 8
    incoming = lax.dynamic_slice_in_dim(illumination, top_index, 1, 0)
    target = lax.dynamic_slice_in_dim(observed, top_index, 1, 0)
    adjoint = complex_mul(whole_map, incoming) - target
    for former, latter, forward_inv, backward_inv, side_flag in reversed(saved):
        west_side, east_side = descend_pair(
            former, latter, forward_inv, backward_inv, incoming, adjoint
        )
        if side_flag is None:
            incoming = alternate(west_side[0], east_side[0])
            adjoint = alternate(west_side[1], east_side[1])
        else:
            incoming = jnp.where(side_flag == 0, west_side[0], east_side[0])
            adjoint = jnp.where(side_flag == 0, west_side[1], east_side[1])
    conj_adjoint = jnp.stack([adjoint[..., 0, :, :], -adjoint[..., 1, :, :]], axis=-3)
    lifted = complex_mul(lift_rows, conj_adjoint)
    probed = complex_mul(probe_rows, incoming)
    contrib = lifted[:, :, 0] * probed[:, :, 0] - lifted[:, :, 1] * probed[:, :, 1]
    partial_grad = jnp.einsum("lfks,f->lk", contrib, squared, precision=highest)
    total = lax.psum(partial_grad, "freq")
    rows_here = jnp.arange(lax.axis_size("box") * leaf_count, dtype=jnp.int32)
    chooser = (rows_here[:, None] == mine_order[None, :]).astype(jnp.float32)
    return lax.psum_scatter(
        jnp.matmul(chooser, total, precision=highest), "box", scatter_dimension=0, tiled=True
    )


H = 128
MESH = pl.DeviceIdType.MESH
F32 = jnp.float32


def halves(x):
    high = x.astype(jnp.bfloat16)
    return high, (x - high.astype(F32)).astype(jnp.bfloat16)


def mm(a, b):
    dot = partial(jnp.dot, preferred_element_type=F32)
    return dot(a[0], b[0]) + (dot(a[0], b[1]) + dot(a[1], b[0]))


def blk(x):
    turned = jnp.concatenate([-x[H:], x[:H]], axis=0)
    return jnp.concatenate([x, turned], axis=1)


def apply_iterate(op, x):
    once = mm(op, halves(x))
    even = x + mm(op, halves(once))
    return even + mm(op, halves(even))


def pack(x):
    q = x.shape[0] // 4
    return jnp.concatenate([x[i * q : (i + 1) * q] for i in range(4)], axis=1)


def unpack(x):
    q = x.shape[1] // 4
    return jnp.concatenate([x[:, i * q : (i + 1) * q] for i in range(4)], axis=0)


def adjoint_maps(a13, a33, b23, b33):
    op_a33, op_a13, op_b23 = halves(blk(a33)), halves(blk(a13)), halves(blk(b23))
    split_b33, split_a33 = halves(b33), halves(a33)
    coupled = mm(op_a33, split_b33)
    op = halves(blk(coupled))
    row = lax.broadcasted_iota(jnp.int32, (2 * H, H), 0)
    col = lax.broadcasted_iota(jnp.int32, (2 * H, H), 1)
    even = jnp.where(row == col, 1.0, 0.0) + mm(op, halves(coupled))
    inverse = halves(even + mm(op, halves(even)))
    f1 = blk(mm(halves(blk(mm(op_a13, split_b33))), inverse))
    f2 = blk(mm(op_b23, inverse))
    g1 = blk(a13 + mm(halves(f1), split_a33))
    g2 = blk(mm(halves(f2), split_a33))
    to_l3 = jnp.concatenate([f1.T, f2.T], axis=1)
    to_k3 = jnp.concatenate([g1.T, g2.T], axis=1)
    return to_l3, to_k3


def incoming_maps(op_a33, op, b33a31, a31, b32):
    reach = apply_iterate(op, jnp.concatenate([b33a31, b32], axis=1))
    echo = mm(op_a33, halves(reach))
    return reach, jnp.concatenate([echo[:, :H] + a31, echo[:, H:]], axis=1)


def wide(x):
    return jnp.concatenate([blk(x[:, :H]), blk(x[:, H:])], axis=1)


def store_halves(ref, x):
    high, low = halves(x)
    ref[0] = high
    ref[1] = low


def load_halves(ref):
    return ref[0], ref[1]


def kernel(
    base, lift, probe, wave_in, contrast, order_in, illum_in, observed_in, out,
    wave, order, illum, observed, opl, opr, oprt, evec, gvec, es_sem, er_sem,
    lbuf, pbuf, bbuf, cbuf, own, got, t33, tvec, mbuf, vbuf, inc1, adj1, inc2, adj2,
    gpart, grecv, loc_sem, xs_sem, xr_sem, cs_sem, cr_sem, zs_sem, zr_sem,
    ts_sem, tr_sem, us_sem, ur_sem, ms_sem, mr_sem, vs_sem, vr_sem, gs_sem, gr_sem,
):
    box = lax.axis_index("box")
    row = lax.axis_index("row")
    core = lax.axis_index("freq")
    side = lax.rem(box, 2)
    pair = box // 2
    mate = box + 1 - 2 * side
    other = 1 - row
    boxes = [lax.rem(box + d, 4) for d in (1, 2, 3)]
    peers = [{"row": other, "freq": core}, {"row": row, "freq": 1 - core}, {"row": other, "freq": 1 - core}]

    def remote(source, target, sender, receiver, where):
        return pltpu.make_async_remote_copy(
            src_ref=source, dst_ref=target, send_sem=sender, recv_sem=receiver,
            device_id=where, device_id_type=MESH,
        )

    mine = pl.ds(pl.multiple_of(row * H, H), H)
    theirs = pl.ds(pl.multiple_of(other * H, H), H)
    loads = []
    for leaf in range(2):
        loads += [
            (lift.at[leaf, row], lbuf.at[leaf, :, mine, :]),
            (probe.at[leaf, row], pbuf.at[leaf, :, mine, :]),
            (base.at[leaf, row], bbuf.at[leaf]),
        ]
    loads += [(wave_in, wave), (order_in, order), (illum_in.at[0, row], illum)]
    loads += [(observed_in.at[0, row], observed), (contrast, cbuf.at[box, row])]
    loads = [pltpu.make_async_copy(s, t, loc_sem.at[i]) for i, (s, t) in enumerate(loads)]
    for load in loads:
        load.start()

    barrier = pltpu.get_barrier_semaphore()
    others = []
    for d in (2, 1, 3, 0):
        for i in range(2):
            for j in range(2):
                if d + i + j > 0:
                    place = lax.rem(box + d, 4), lax.rem(row + i, 2), lax.rem(core + j, 2)
                    others.append(dict(zip(("box", "row", "freq"), place)))
    for where in others:
        pl.semaphore_signal(barrier, inc=1, device_id=where, device_id_type=MESH)
    pl.semaphore_wait(barrier, 15)

    early = remote(contrast, cbuf.at[box, row], xs_sem.at[8], xr_sem.at[8], peers[0])
    early.start()
    low, high = pl.ds(0, H), pl.ds(H, H)
    plan = [(lift, lbuf, 0, high), (probe, pbuf, 0, high), (lift, lbuf, 1, high), (probe, pbuf, 1, high)]
    plan += [(probe, pbuf, 0, low), (probe, pbuf, 1, low), (lift, lbuf, 0, low), (lift, lbuf, 1, low)]
    sends, waits = [early], []
    for i, (source, target, leaf, cols) in enumerate(plan):
        copy = remote(
            source.at[leaf, other, :, :, cols], target.at[leaf, :, mine, cols],
            xs_sem.at[i], xr_sem.at[i], peers[0],
        )
        copy.start()
        sends.append(copy)
        waits.append(
            remote(
                source.at[leaf, other, :, :, cols], target.at[leaf, :, theirs, cols],
                xs_sem.at[i], xr_sem.at[i], peers[0],
            )
        )

    for load in loads:
        load.wait()
    remote(contrast, cbuf.at[box, other], xs_sem.at[8], xr_sem.at[8], peers[0]).wait_recv()
    for d in range(3):
        copy = remote(cbuf.at[box], cbuf.at[box], cs_sem.at[d], cr_sem.at[box], {"box": boxes[d]})
        copy.start()
        sends.append(copy)
    for d in range(3):
        slot = cbuf.at[boxes[d]]
        remote(slot, slot, cs_sem.at[d], cr_sem.at[boxes[d]], {"box": boxes[d]}).wait_recv()
    number = wave[row]
    squared = number * number
    weight = []
    for leaf in range(2):
        stored = order[box * 2 + leaf]
        total = jnp.zeros((2, H), F32)
        for j in range(8):
            total = total + jnp.where(stored == j, cbuf[j // 2, :, j % 2, :], 0.0)
        total = total * squared
        weight.append(
            jnp.concatenate([jnp.broadcast_to(total[i : i + 1], (H, H)).T for i in range(2)], axis=0)
        )

    for copy in waits[:4]:
        copy.wait_recv()

    def lift_op(leaf, cols):
        real, imag = lbuf[leaf, 0, :, cols].T, lbuf[leaf, 1, :, cols].T
        upper = jnp.concatenate([real, -imag], axis=1)
        return halves(jnp.concatenate([upper, jnp.concatenate([imag, real], axis=1)], axis=0))

    def weighted(leaf, cols):
        both = [pbuf[leaf, part, :, cols] * weight[leaf] for part in range(2)]
        return halves(jnp.concatenate(both, axis=0))

    def based(leaf, rows, cols):
        return jnp.concatenate([bbuf[leaf, 0, rows, cols], bbuf[leaf, 1, rows, cols]], axis=0)

    op3 = [lift_op(leaf, high) for leaf in range(2)]
    w3 = [weighted(leaf, high) for leaf in range(2)]
    a33, b33 = [based(leaf, high, high) + mm(op3[leaf], w3[leaf]) for leaf in range(2)]
    op_a33, op_b33 = halves(blk(a33)), halves(blk(b33))
    op = halves(blk(mm(op_b33, halves(a33))))
    for copy in waits[4:6]:
        copy.wait_recv()
    w1 = [weighted(leaf, low) for leaf in range(2)]
    a31, b32 = [based(leaf, high, low) + mm(op3[leaf], w1[leaf]) for leaf in range(2)]
    reach, echo = incoming_maps(op_a33, op, mm(op_b33, halves(a31)), a31, b32)
    for copy in waits[6:]:
        copy.wait_recv()
    op1 = [lift_op(leaf, low) for leaf in range(2)]
    a13, b23 = [based(leaf, low, high) + mm(op1[leaf], w3[leaf]) for leaf in range(2)]
    a11, b22 = [based(leaf, low, low) + mm(op1[leaf], w1[leaf]) for leaf in range(2)]
    bottom = mm(halves(blk(b23)), halves(echo))
    top = mm(halves(blk(a13)), halves(reach))
    top_left, top_right = top[:, :H] + a11, top[:, H:]
    low_left, low_right = bottom[:, :H], bottom[:, H:] + b22
    own[0] = low_right
    own[1] = low_left
    own[2] = top_right
    def illum_half(ref, part):
        rows = pl.ds(part * H, H)
        return jnp.concatenate([ref[0, :, rows].T, ref[1, :, rows].T], axis=0)

    i1, j2 = illum_half(illum, 0), illum_half(illum, 1)
    upper_pair = pair == 1
    east = side == 1
    given = jnp.where(upper_pair, j2, i1)

    swaps = [remote(own.at[i], got.at[i], zs_sem.at[i], zr_sem.at[i], {"box": mate}) for i in range(3)]
    ahead = remote(evec, gvec, es_sem, er_sem, {"box": mate})
    sends += swaps
    swaps[0].start()

    @pl.when(side == 0)
    def _():
        evec[...] = pack(mm(halves(blk(low_left)), halves(given)))
        ahead.start()

    @pl.when(east)
    def _():
        swaps[1].start()

    store_halves(inc1.at[0], wide(reach))
    store_halves(inc1.at[1], wide(echo))
    to_l3, to_k3 = adjoint_maps(a13, a33, b23, b33)
    store_halves(adj1.at[0], to_l3)
    store_halves(adj1.at[1], to_k3)

    @pl.when(side == 0)
    def _():
        swaps[1].start()

    swaps[2].start()

    swaps[0].wait_recv()
    a33, b33 = jnp.where(east, got[0], low_right), jnp.where(east, low_right, got[0])
    op_a33, op_b33 = halves(blk(a33)), halves(blk(b33))
    op = halves(blk(mm(op_b33, halves(a33))))
    far, mid, first = {"box": 4 - box}, {"box": 2}, {"box": 0}
    tops = []
    for i, (where, slot) in enumerate([(far, pair), (mid, pair), (first, 0), (first, 1)]):
        tops.append(
            [
                remote(t33.at[slot], t33.at[slot], ts_sem.at[i], tr_sem.at[slot], where),
                remote(tvec.at[slot], tvec.at[slot], us_sem.at[i], ur_sem.at[slot], where),
            ]
        )

    @pl.when(east)
    def _():
        ahead.wait_recv()
        enter = unpack(gvec[...])
        seen = jnp.concatenate([low_left, mm(op_b33, halves(enter))], axis=1)
        seen = mm(op_a33, halves(apply_iterate(op, seen)))
        seen = jnp.concatenate([seen[:, :H], seen[:, H:] + enter], axis=1)
        seen = mm(halves(blk(top_right)), halves(seen))
        t33[pair] = seen[:, :H] + top_left
        tvec[pair] = pack(seen[:, H:])
        for copy in tops[0]:
            copy.start()

    @pl.when(box == 1)
    def _():
        for copy in tops[2]:
            copy.start()

    swaps[1].wait_recv()
    a31, b32 = jnp.where(east, got[1], low_left), jnp.where(east, low_left, got[1])
    reach, echo = incoming_maps(op_a33, op, mm(op_b33, halves(a31)), a31, b32)

    @pl.when(east)
    def _():
        for copy in tops[1]:
            copy.start()

    @pl.when(side == 0)
    def _():
        half_map = mm(halves(blk(top_right)), halves(reach))
        right = blk(half_map[:, H:])
        store_halves(opl, blk(half_map[:, :H] + top_left))
        store_halves(opr, right)
        store_halves(oprt, right.T)

    @pl.when(box == 1)
    def _():
        for copy in tops[3]:
            copy.wait_recv()
            copy.start()

    store_halves(inc2, wide(jnp.where(east, echo, reach)))
    swaps[2].wait_recv()
    a13, b23 = jnp.where(east, got[2], top_right), jnp.where(east, top_right, got[2])
    to_l3, to_k3 = adjoint_maps(a13, a33, b23, b33)
    store_halves(adj2, jnp.where(east, to_k3, to_l3))

    for s in range(2):

        @pl.when(side == 0 if s else box != 1)
        def _():
            where = {"box": boxes[0]}
            remote(t33.at[s], t33.at[s], ts_sem.at[0], tr_sem.at[s], where).wait_recv()
            remote(tvec.at[s], tvec.at[s], us_sem.at[0], ur_sem.at[s], where).wait_recv()

    a33, b33 = t33[0], t33[1]
    enter = unpack(tvec[0])
    full_a33, full_b33 = blk(a33), blk(b33)
    op_a33, op_b33 = halves(full_a33), halves(full_b33)
    op = halves(blk(mm(op_b33, halves(a33))))
    i3 = apply_iterate(op, mm(op_b33, halves(enter)) + unpack(tvec[1]))
    j3 = enter + mm(op_a33, halves(i3))
    inner = jnp.where(upper_pair, j3, i3)

    @pl.when(side == 0)
    def _():
        goal = jnp.where(upper_pair, illum_half(observed, 1), illum_half(observed, 0))
        misfit = mm(load_halves(opl), halves(given)) + mm(load_halves(opr), halves(inner)) - goal
        mbuf[...] = pack(misfit)
        vbuf[pair] = pack(mm(load_halves(oprt), halves(misfit)))
        for d in range(3):
            remote(vbuf.at[pair], vbuf.at[pair], vs_sem.at[d], vr_sem.at[pair], {"box": boxes[d]}).start()
        remote(mbuf, mbuf, ms_sem, mr_sem, {"box": mate}).start()

    flip_a33, flip_b33 = full_a33.T, full_b33.T
    op_at, op_bt = halves(flip_a33), halves(flip_b33)
    op = halves(blk(mm(op_bt, halves(flip_a33[:, :H]))))

    for s in range(2):

        @pl.when(box != 2 * s)
        def _():
            remote(vbuf.at[s], vbuf.at[s], vs_sem.at[0], vr_sem.at[s], {"box": boxes[0]}).wait_recv()

    crossed = unpack(vbuf[0])
    l3 = apply_iterate(op, mm(op_bt, halves(crossed)) + unpack(vbuf[1]))
    k3 = crossed + mm(op_at, halves(l3))

    @pl.when(east)
    def _():
        remote(mbuf, mbuf, ms_sem, mr_sem, {"box": mate}).wait_recv()

    back = unpack(mbuf[...])
    below = jnp.where(upper_pair, k3, l3)
    inner_in = mm(load_halves(inc2), halves(jnp.concatenate([given, inner], axis=0)))
    inner_back = mm(load_halves(adj2), halves(jnp.concatenate([back, below], axis=0)))
    in_outer = jnp.where(east, inner, given)
    back_outer = jnp.where(east, below, back)
    split_in = halves(jnp.concatenate([in_outer, inner_in], axis=0))
    split_back = halves(jnp.concatenate([back_outer, inner_back], axis=0))

    ones = jnp.ones((8, 32), jnp.bfloat16)
    across = (((1,), (1,)), ((), ()))
    for leaf in range(2):
        outer_in = inner_in if leaf else in_outer
        outer_back = inner_back if leaf else back_outer
        leaf_in = mm(load_halves(inc1.at[leaf]), split_in)
        leaf_back = mm(load_halves(adj1.at[leaf]), split_back)
        in_re = jnp.concatenate([outer_in[:H], leaf_in[:H]], axis=0)
        in_im = jnp.concatenate([outer_in[H:], leaf_in[H:]], axis=0)
        back_re = jnp.concatenate([outer_back[:H], leaf_back[:H]], axis=0)
        back_im = jnp.concatenate([outer_back[H:], leaf_back[H:]], axis=0)
        probe_in = jnp.concatenate(
            [jnp.concatenate([in_re, in_im], axis=1), jnp.concatenate([-in_im, in_re], axis=1)], axis=0
        )
        lift_in = jnp.concatenate(
            [jnp.concatenate([back_re, -back_im], axis=1), jnp.concatenate([back_im, back_re], axis=1)], axis=0
        )
        lifted = mm(halves(jnp.concatenate([lbuf[leaf, 0], lbuf[leaf, 1]], axis=1)), halves(lift_in))
        probed = mm(halves(jnp.concatenate([pbuf[leaf, 0], pbuf[leaf, 1]], axis=1)), halves(probe_in))
        contrib = lifted[:, :32] * probed[:, :32] - lifted[:, 32:] * probed[:, 32:]
        contrib = halves(contrib * squared)
        summed = [lax.dot_general(ones, part, across, preferred_element_type=F32) for part in contrib]
        summed = summed[0] + summed[1]
        gpart[0, leaf : leaf + 1, :] = summed[0:1, :H]
        gpart[1, leaf : leaf + 1, :] = summed[0:1, H:]

    place = box * 4 + row * 2 + core
    grecv[place] = gpart[row]
    ends = []
    for i, where in enumerate(others):
        copy = remote(gpart.at[where["row"]], grecv.at[place], gs_sem.at[i], gr_sem.at[place], where)
        copy.start()
        sends.append(copy)
        source = where["box"] * 4 + where["row"] * 2 + where["freq"]
        ends.append(remote(grecv.at[source], grecv.at[source], gs_sem.at[i], gr_sem.at[source], where))
    for copy in ends:
        copy.wait_recv()
    sums = []
    for b in range(4):
        sums.append((grecv[4 * b] + grecv[4 * b + 1]) + (grecv[4 * b + 2] + grecv[4 * b + 3]))
    for j in range(2):
        total = jnp.zeros((1, H), F32)
        for t in range(8):
            total = total + jnp.where(order[t] == box * 2 + j, sums[t // 2][t % 2 : t % 2 + 1, :], 0.0)
        out[j : j + 1, :] = total

    for copy in sends:
        copy.wait_send()

    @pl.when(east)
    def _():
        for copy in tops[0] + tops[1]:
            copy.wait_send()

    @pl.when(box == 1)
    def _():
        for copy in tops[2] + tops[3]:
            copy.wait_send()

    @pl.when(side == 0)
    def _():
        for d in range(3):
            remote(vbuf.at[pair], vbuf.at[pair], vs_sem.at[d], vr_sem.at[pair], {"box": boxes[d]}).wait_send()
        remote(mbuf, mbuf, ms_sem, mr_sem, {"box": mate}).wait_send()
        ahead.wait_send()


def fused(*args):
    half = jnp.bfloat16
    dma = pltpu.SemaphoreType.DMA
    scratch = [
        pltpu.SMEM((2,), F32),
        pltpu.SMEM((8,), jnp.int32),
        pltpu.VMEM((2, 32, 2 * H), F32),
        pltpu.VMEM((2, 32, 2 * H), F32),
        pltpu.VMEM((2, 2 * H, 2 * H), half),
        pltpu.VMEM((2, 2 * H, 2 * H), half),
        pltpu.VMEM((2, 2 * H, 2 * H), half),
        pltpu.VMEM((H // 2, H), F32),
        pltpu.VMEM((H // 2, H), F32),
        dma(()),
        dma(()),
        pltpu.VMEM((2, 2, 2 * H, 2 * H), F32),
        pltpu.VMEM((2, 2, 2 * H, 2 * H), F32),
        pltpu.VMEM((2, 2, 2 * H, 2 * H), F32),
        pltpu.VMEM((4, 2, 2, H), F32),
        pltpu.VMEM((3, 2 * H, H), F32),
        pltpu.VMEM((3, 2 * H, H), F32),
        pltpu.VMEM((2, 2 * H, H), F32),
        pltpu.VMEM((2, H // 2, H), F32),
        pltpu.VMEM((H // 2, H), F32),
        pltpu.VMEM((2, H // 2, H), F32),
        pltpu.VMEM((2, 2, 2 * H, 4 * H), half),
        pltpu.VMEM((2, 2, 2 * H, 4 * H), half),
        pltpu.VMEM((2, 2 * H, 4 * H), half),
        pltpu.VMEM((2, 2 * H, 4 * H), half),
        pltpu.VMEM((2, 2, H), F32),
        pltpu.VMEM((16, 2, H), F32),
        dma((11,)), dma((9,)), dma((9,)), dma((3,)), dma((4,)), dma((3,)), dma((3,)),
        dma((4,)), dma((2,)), dma((4,)), dma((2,)), dma(()), dma(()), dma((3,)), dma((2,)),
        dma((15,)), dma((16,)),
    ]
    hbm, vmem = [pl.BlockSpec(memory_space=space) for space in (pltpu.HBM, pltpu.VMEM)]
    return pl.pallas_call(
        kernel,
        out_shape=jax.ShapeDtypeStruct((2, H), F32),
        in_specs=[hbm] * 8,
        out_specs=vmem,
        scratch_shapes=scratch,
        compiler_params=pltpu.CompilerParams(
            collective_id=0, has_side_effects=True, vmem_limit_bytes=63 * 2**20
        ),
        name="gradient",
    )(*args[:6], *[jnp.swapaxes(x, -1, -2) for x in args[6:]])


def pick(mesh):
    def local(*args):
        shape = mesh.shape
        fits = shape["box"] == 4 and shape["row"] == 2 and shape["freq"] == 2
        fits = fits and args[0].shape == (2, 2, 2, 256, 256) and args[6].shape == (1, 2, 2, 256, 32)
        return (fused if fits else body)(*args)

    return local


def solution(mesh):
    return jax.shard_map(
        pick(mesh),
        mesh=mesh,
        in_specs=(
            P(("group", "box"), "freq", None, None, None),
            P(("group", "box"), "freq", None, "row", None),
            P(("group", "box"), "freq", None, "row", None),
            P(("group", "freq")),
            P(("group", "box"), "row"),
            P("group"),
            P("group", "freq", None, None, None),
            P("group", "freq", None, None, None),
        ),
        out_specs=P(("group", "box"), "row"),
        check_vma=False,
    )
```
